512 devices in a mesh: dp: 64 (over y_hi, z, x), tensor: 8 (over y_lo, core).
Axes of the slice: x: 4, y: 8 (y_hi: 2, y_lo: 4; y = y_hi * 4 + y_lo), z: 8, core: 2. Of those that a mesh axis runs over, the one named last changes fastest.
Arguments:
- acts: bfloat16 [2, 8192, 8192], P(None, ('dp', 'tensor')), may hold values from -6 to 6
- grad_out: bfloat16 [2, 8192, 8192], P(None, ('dp', 'tensor')), may hold values from -24 to 24
- w_gate: bfloat16 [8192, 128], P(None, 'tensor'), may hold values from -0.0625 to 0.0625
- w_up: bfloat16 [8192, 128], P(None, 'tensor'), may hold values from -0.0625 to 0.0625
- w_down: bfloat16 [128, 8192], P('tensor'), may hold values from -0.5 to 0.5
- overflow: int32 [64, 2], P('dp'), may hold values 0 or 1
- step: int32 [1], replicated, may hold values from 1 to 8
- master: float32 [3, 128, 8192], P(None, 'tensor', 'dp'), may hold values from -0.75 to 0.75
- moment1: float32 [3, 128, 8192], P(None, 'tensor', 'dp'), may hold values from -6 to 6
- moment2: float32 [3, 128, 8192], P(None, 'tensor', 'dp'), may hold values from 0.01 to 1
Outputs:
- new_master: float32 [3, 128, 8192], P(None, 'tensor', 'dp')
- new_moment1: float32 [3, 128, 8192], P(None, 'tensor', 'dp')
- new_moment2: float32 [3, 128, 8192], P(None, 'tensor', 'dp')
The draws below stay inside these ranges and needn't reach their ends.
All inputs are finite; a program needn't handle non-finite values. No bound on the sum of `overflow` on one device may be relied on, other than what follows from the above.
Results may differ from the reference program's by a relative error of at most 0.0033.
Values may be sent and summed in bfloat16 or wider, within the bound.
A program may use at most 64 MiB of HBM per device.

```python
import math
import jax
import jax.numpy as jnp

D = 8192
MB = 2
HIDW = 128
TOK = 128
ROWS = 8192
N_DP = 64


def touch_ends(array, key, least, high):
    longest = array.shape.index(max(array.shape))
    spots = []
    for shift in (0, 1):
        where = [jax.random.randint(jax.random.fold_in(key, axis), (), 0, length) for axis, length in enumerate(array.shape)]
        where[longest] = (where[longest] + shift) % array.shape[longest]
        spots.append(tuple(where))
    return array.at[spots[0]].set(least).at[spots[1]].set(high)


def with_spikes(values, stream_key, source, target, shards_of, factor):
    def block_of(position):
        return (jnp.arange(values.shape[position]) // (values.shape[position] // shards_of)).reshape((-1,) + (1,) * (values.ndim - 1 - position))

    near = jax.random.permutation(stream_key, shards_of)[block_of(target)]
    second = (block_of(target) + shards_of // 2) % shards_of
    return jnp.where((block_of(source) == near) | (block_of(source) == second), factor * values, values)


def shard_levels(stream_key, shape, shards, smallest, top_value):
    level = 1.0
    for position, shards_of in shards:
        heights = jax.random.uniform(jax.random.fold_in(jax.random.fold_in(stream_key, 6), position), (shards_of,), jnp.float32, smallest / len(shards), top_value / len(shards))
        level = level * jnp.repeat(jnp.exp(heights), shape[position] // shards_of).reshape((-1,) + (1,) * (len(shape) - 1 - position))
    return level


def noise(stream_key, extent, width, bound, cuts=(), kind=jnp.bfloat16):
    loudness = shard_levels(stream_key, extent, cuts, -0.22, 0.18) if cuts else 1.0
    result = jax.random.normal(stream_key, extent, jnp.float32) * width * loudness
    return jnp.minimum(jnp.maximum(result, -bound), bound).astype(kind)


def heavy_noise(rng, dims, scale, most, pieces, heavy, dtype=jnp.bfloat16):
    values = scale * jax.random.normal(rng, dims, jnp.float32)
    if pieces:
        values = values * shard_levels(rng, dims, pieces, -0.22, 0.18)
    return jnp.clip(with_spikes(values, jax.random.fold_in(rng, 3), *heavy), -most, most).astype(dtype)


def setup_inputs(seed: int = 0) -> dict:
    arg_keys = jax.random.split(jax.random.key(seed), 11)
    return {
        "acts": noise(arg_keys[0], (MB, ROWS, D), 1.0, 6.0, ((1, 512),)),
        "grad_out": heavy_noise(arg_keys[1], (MB, ROWS, D), 1.0, 24.0, ((1, 512),), (1, 2, 512, 6.0)),
        "w_gate": noise(arg_keys[2], (D, HIDW), D ** -0.5, 0.0625, ((1, 8),)),
        "w_up": noise(arg_keys[3], (D, HIDW), D ** -0.5, 0.0625, ((1, 8),)),
        "w_down": noise(arg_keys[4], (HIDW, D), HIDW ** -0.5, 0.5, ((0, 8),)),
        "overflow": touch_ends((jax.random.randint(arg_keys[5], (N_DP, MB), 0, 4) < 1).astype(jnp.int32), jax.random.fold_in(arg_keys[5], 1), 0, 1),
        "step": jax.random.randint(arg_keys[6], (1,), 1, 9).astype(jnp.int32),
        "master": noise(arg_keys[7], (3, HIDW, D), 0.05, 0.75, ((1, 8), (2, 64)), jnp.float32),
        "moment1": noise(arg_keys[8], (3, HIDW, D), 0.5, 6.0, ((1, 8), (2, 64)), jnp.float32),
        "moment2": jnp.clip(jnp.exp(math.log(1.0) - 4.6051702 * jax.random.uniform(arg_keys[9], (3, HIDW, D), jnp.float32) ** shard_levels(arg_keys[9], (3, HIDW, D), ((1, 8), (2, 64)), -0.2, 0.2)), 0.01, 1.0),
    }


def reference(acts, grad_out, w_gate, w_up, w_down, overflow, step, master, moment1, moment2):
    good = (1 - overflow).T
    mask = jnp.repeat(good, TOK, axis=1) > 0
    total = jnp.zeros((3, HIDW, D), jnp.float32)
    for index in range(MB):
        rows_x = acts[index]
        rows_dy = grad_out[index]
        gate = jnp.dot(rows_x, w_gate, preferred_element_type=jnp.float32)
        up = jnp.dot(rows_x, w_up, preferred_element_type=jnp.float32)
        sig = jax.nn.sigmoid(gate)
        silu = gate * sig
        hidden = (silu * up).astype(jnp.bfloat16)
        dh = jnp.dot(rows_dy, w_down.T, preferred_element_type=jnp.float32)
        dup = (dh * silu).astype(jnp.bfloat16)
        dgate = (dh * up * sig * (1.0 + gate * (1.0 - sig))).astype(jnp.bfloat16)
        keep_rows = mask[index][:, None]
        zero = jnp.zeros((), jnp.bfloat16)
        hidden = jnp.where(keep_rows, hidden, zero)
        dup = jnp.where(keep_rows, dup, zero)
        dgate = jnp.where(keep_rows, dgate, zero)
        g_gate = jnp.dot(dgate.T, rows_x, preferred_element_type=jnp.float32)
        g_up = jnp.dot(dup.T, rows_x, preferred_element_type=jnp.float32)
        g_down = jnp.dot(hidden.T, rows_dy, preferred_element_type=jnp.float32)
        total = total + jnp.stack([g_gate, g_up, g_down])
    grad = total / jnp.float32(MB * N_DP)
    count = jnp.sum(overflow).astype(jnp.float32)
    keep = 1.0 - count / jnp.float32(MB * N_DP)
    new_moment1 = 0.9 * moment1 + 0.1 * grad
    new_moment2 = 0.95 * moment2 + 0.05 * grad * grad
    steps_f = step[0].astype(jnp.float32)
    corr1 = 1.0 - jnp.power(jnp.float32(0.9), steps_f)
    corr2 = 1.0 - jnp.power(jnp.float32(0.95), steps_f)
    direction = new_moment1 / corr1 / (jnp.sqrt(new_moment2 / corr2) + 1e-08)
    new_master = master - 0.01 * keep * (direction + 0.1 * master)
    return (new_master, new_moment1, new_moment2)
```

```python
import jax
import jax.numpy as jnp
from jax import lax
from jax.experimental import pallas as pl
from jax.experimental.pallas import tpu as pltpu
from jax.sharding import PartitionSpec as P

X, YH, YL, Z = 4, 2, 4, 8
Y = YH * YL
C = 2
MB, RT = 2, 16
TOK = MB * RT
SLOTS = X * C
LANES = 128
CC = Z * LANES
HID = 128
MESH = pl.DeviceIdType.MESH
NT = (((1,), (1,)), ((), ()))


def dev(y, z, x, c):
    return (lax.div(y, YL) * Z + z) * X + x, lax.rem(y, YL) * C + c


def kernel(
    acts_hbm, dy_hbm, wg_hbm, wu_hbm, wd_hbm, ovf, out,
    acts_v, dy_v, w_v, sx, bx, sw, wb, pt, rx, ab, sz, rz, sy, ry, s2y, r2y, s2z, r2z,
    ld, xs, xr, ws, wr, ps, pr, as_, ar, zs, zr, ys, yr, y2s, y2r, z2s, z2r,
):
    dp, t = lax.axis_index("dp"), lax.axis_index("tensor")
    x = lax.rem(dp, X)
    z = lax.rem(lax.div(dp, X), Z)
    yh = lax.div(dp, X * Z)
    yl = lax.div(t, C)
    c = lax.rem(t, C)
    y = yh * YL + yl
    me = x * C + c
    sib = 1 - c

    loads = [
        pltpu.make_async_copy(src, dst, ld.at[i])
        for i, (src, dst) in enumerate(
            [(acts_hbm, acts_v), (dy_hbm, dy_v), (wg_hbm, w_v.at[0]), (wu_hbm, w_v.at[1]), (wd_hbm, w_v.at[2])]
        )
    ]
    for load in loads:
        load.start()

    barrier = pltpu.get_barrier_semaphore()
    friends = []
    for dx in range(X):
        for dc in range(C):
            if dx or dc:
                friends.append(dev(y, z, lax.rem(x + dx, X), lax.rem(c + dc, C)))
    for step in range(1, Y):
        for dc in range(C):
            friends.append(dev(lax.rem(y + step, Y), z, x, lax.rem(c + dc, C)))
    for step in range(1, Z):
        friends.append(dev(y, lax.rem(z + step, Z), x, c))
    for friend in friends:
        pl.semaphore_signal(barrier, inc=1, device_id=friend, device_id_type=MESH)
    for load in loads:
        load.wait()
    pl.semaphore_wait(barrier, len(friends))

    sends = []

    def send(src, dst, send_sem, recv_sem, where):
        copy = pltpu.make_async_remote_copy(
            src_ref=src, dst_ref=dst, send_sem=send_sem, recv_sem=recv_sem, device_id=where, device_id_type=MESH
        )
        copy.start()
        return copy

    def arrived(dst, sem):
        pltpu.make_async_copy(dst, dst, sem).wait()

    def gather_columns(store, xp, cp):
        for k in range(Z):
            at = pl.ds(pl.multiple_of(((cp * Z + k) * X + xp) * LANES, LANES), LANES)
            store(0, k, acts_v[:, :, at])
            store(1, k, dy_v[:, :, at])

    for dx in [2, 1, 3, 0] if X == 4 else list(range(1, X)) + [0]:
        for dc in range(C):
            if dx == 0 and dc == 0:
                continue
            xp, cp = lax.rem(x + dx, X), lax.rem(c + dc, C)
            n = dx * C + dc

            def store(a, k, value, n=n):
                sx[n, a, :, :, k * LANES : (k + 1) * LANES] = value

            gather_columns(store, xp, cp)
            sends.append(send(sx.at[n], bx.at[:, me], xs.at[n], xr.at[n], dev(y, z, xp, cp)))

    for cp in range(C):
        for k in range(Z):
            at = pl.ds(pl.multiple_of(((cp * Z + k) * X + x) * LANES, LANES), LANES)
            sw[cp, :, :, k * LANES : (k + 1) * LANES] = w_v[:, :, at]
    rows = pl.ds(pl.multiple_of(t * RT, RT), RT)
    half = CC // 2
    hops = [
        (1, slice(0, CC)),
        (Y - 1, slice(0, CC)),
        (2, slice(0, half)),
        (Y - 2, slice(half, CC)),
    ]
    for i, (hop, cols) in enumerate(hops):
        for cp in range(C):
            sends.append(
                send(
                    sw.at[cp, :, :, cols],
                    wb.at[:, rows, cols],
                    ws.at[i * C + cp],
                    wr.at[i * C + c],
                    dev(lax.rem(y + hop, Y), z, x, cp),
                )
            )
    n = len(hops) * C
    sends.append(send(sw.at[sib], wb.at[:, rows, :], ws.at[n], wr.at[n], dev(y, z, x, sib)))
    wb[:, rows, :] = sw[c]

    def store(a, k, value):
        bx[a, me, :, :, k * LANES : (k + 1) * LANES] = value

    gather_columns(store, x, c)

    for i, (hop, cols) in enumerate(hops):
        for cp in range(C):
            arrived(wb.at[:, rows, cols], wr.at[i * C + cp])
    arrived(wb.at[:, rows, :], wr.at[n])

    lost = (ovf[0, 0] + ovf[0, 1]).astype(jnp.float32)
    for dx in [0, 1, 3, 2] if X == 4 else range(X):
        for dc in range(C):
            if dx or dc:
                arrived(bx.at[:, me], xr.at[dx * C + dc])
        g = lax.rem(x - dx + X, X)
        a = bx[0, pl.ds(g * C, C)].reshape(C * TOK, CC)
        d = bx[1, pl.ds(g * C, C)].reshape(C * TOK, CC)
        gate_up = lax.dot_general(a, wb[0:2].reshape(2 * HID, CC), NT, preferred_element_type=jnp.float32)
        dh = lax.dot_general(d, wb[2], NT, preferred_element_type=jnp.float32)
        for cc in range(C):
            part = slice(cc * TOK, (cc + 1) * TOK)
            pt[g * C + cc, 0:TOK] = gate_up[part, :HID]
            pt[g * C + cc, TOK : 2 * TOK] = gate_up[part, HID:]
            pt[g * C + cc, 2 * TOK : 3 * TOK] = dh[part]
            pt[g * C + cc, 3 * TOK :] = jnp.full((8, LANES), lost, jnp.float32)
        for dc in range(C):
            if dx or dc:
                cp = lax.rem(c + dc, C)
                n = dx * C + dc
                sends.append(send(pt.at[g * C + cp], rx.at[me], ps.at[n], pr.at[n], dev(y, z, g, cp)))
    rx[me] = pt[me]
    for n in range(1, SLOTS):
        arrived(rx.at[me], pr.at[n])
    total = rx[0]
    for n in range(1, SLOTS):
        total = total + rx[n]
    gate, up, dh = total[0:TOK], total[TOK : 2 * TOK], total[2 * TOK : 3 * TOK]
    count = total[3 * TOK :]
    sig = 1.0 / (1.0 + jnp.exp(-gate))
    silu = gate * sig
    first = lax.broadcasted_iota(jnp.int32, (TOK, HID), 0) < RT
    keep_rows = jnp.where(first, 1 - ovf[0, 0], 1 - ovf[0, 1]) > 0
    zero = jnp.zeros((TOK, HID), jnp.float32)
    ab[me, 0] = jnp.where(keep_rows, dh * up * sig * (1.0 + gate * (1.0 - sig)), zero).astype(jnp.bfloat16)
    ab[me, 1] = jnp.where(keep_rows, dh * silu, zero).astype(jnp.bfloat16)
    ab[me, 2] = jnp.where(keep_rows, silu * up, zero).astype(jnp.bfloat16)
    for dx in range(X):
        for dc in range(C):
            if dx or dc:
                n = dx * C + dc
                where = dev(y, z, lax.rem(x + dx, X), lax.rem(c + dc, C))
                sends.append(send(ab.at[me], ab.at[me], as_.at[n], ar.at[n], where))
    for n in range(1, SLOTS):
        arrived(ab.at[me], ar.at[n])

    lhs = [jnp.transpose(ab[:, k].reshape(SLOTS * TOK, HID)) for k in range(3)]
    lhs_gu = jnp.concatenate(lhs[:2], axis=0)
    wide = 2 * LANES
    for zt in range(Z // 2):
        cols = slice(zt * wide, (zt + 1) * wide)
        acts_cols = bx[0, :, :, :, cols].reshape(SLOTS * TOK, wide)
        dy_cols = bx[1, :, :, :, cols].reshape(SLOTS * TOK, wide)
        gu = jnp.dot(lhs_gu, acts_cols, preferred_element_type=jnp.float32)
        dn = jnp.dot(lhs[2], dy_cols, preferred_element_type=jnp.float32)
        for k, block in enumerate([gu[:HID], gu[HID:], dn]):
            pair = [block[:, :LANES], block[:, LANES:]]
            for b in range(2):
                low = [pair[b][i * RT : i * RT + 8] for i in range(YL * C)]
                sz[zt * 2 + b, k * 64 : (k + 1) * 64] = jnp.concatenate(low, axis=0).astype(jnp.bfloat16)
            for i in range(YL * C):
                high = [p[i * RT + 8 : (i + 1) * RT] for p in pair]
                at = k * 8 * Z + zt * 16
                sy[i, at : at + 16] = jnp.concatenate(high, axis=0).astype(jnp.bfloat16)
    for k in range(Z):
        sz[k, 192:208] = jnp.concatenate([count, count], axis=0).astype(jnp.bfloat16)

    same = c == yh

    def to_y(buf, slots, send_sems, recv_sems):
        for rel in range(1, YL * C):
            i = lax.rem(t + rel, YL * C)
            where = dev(c * YL + lax.div(i, C), z, x, lax.rem(i, C))
            sends.append(send(buf.at[i], slots.at[y], send_sems.at[rel], recv_sems.at[y], where))

        @pl.when(same)
        def _():
            slots[y] = buf[t]

        @pl.when(jnp.logical_not(same))
        def _():
            send(buf.at[t], slots.at[y], send_sems.at[0], recv_sems.at[y], dev(c * YL + yl, z, x, c))

    def from_y(buf, slots, send_sems, recv_sems):
        for rel in range(1, Y):
            arrived(slots.at[y], recv_sems.at[lax.rem(y + rel, Y)])

        @pl.when(jnp.logical_not(same))
        def _():
            arrived(slots.at[y], recv_sems.at[y])
            pltpu.make_async_copy(buf.at[t], buf.at[t], send_sems.at[0]).wait()

    def to_z(buf, slots, send_sems, recv_sems):
        for rel in range(1, Z):
            zp = lax.rem(z + rel, Z)
            sends.append(send(buf.at[zp], slots.at[z], send_sems.at[rel], recv_sems.at[rel], dev(y, zp, x, c)))
        slots[z] = buf[z]

    def from_z(slots, recv_sems):
        for rel in range(1, Z):
            arrived(slots.at[z], recv_sems.at[rel])

    def added(slots, length):
        value = slots[0].astype(jnp.float32)
        for n in range(1, length):
            value = value + slots[n].astype(jnp.float32)
        return value

    to_y(sy, ry, ys, yr)
    to_z(sz, rz, zs, zr)
    from_y(sy, ry, ys, yr)
    high = added(ry, Y)
    for k in range(Z):
        for m in range(3):
            at = m * 8 * Z + k * 8
            s2z[k, m * 8 : (m + 1) * 8] = high[at : at + 8]
    to_z(s2z, r2z, z2s, z2r)
    from_z(rz, zr)
    low = added(rz, Z)
    for i in range(YL * C):
        for m in range(3):
            s2y[i, m * 8 : (m + 1) * 8] = low[m * 64 + i * 8 : m * 64 + (i + 1) * 8]
        s2y[i, 24:32] = low[192:200]
    to_y(s2y, r2y, y2s, y2r)
    from_z(r2z, z2r)
    high = added(r2z, Z)
    from_y(s2y, r2y, y2s, y2r)
    low = added(r2y, Y)
    for m in range(3):
        out[m * 16 : m * 16 + 8] = low[m * 8 : (m + 1) * 8]
        out[m * 16 + 8 : (m + 1) * 16] = high[m * 8 : (m + 1) * 8]
    out[48:56] = low[24:32]

    for copy in sends:
        copy.wait_send()


def reduced_grads(acts, grad_out, w_gate, w_up, w_down, overflow):
    d = acts.shape[2]
    bf16, f32 = jnp.bfloat16, jnp.float32
    hbm = pl.BlockSpec(memory_space=pl.ANY)
    dma = pltpu.SemaphoreType.DMA
    return pl.pallas_call(
        kernel,
        out_shape=jax.ShapeDtypeStruct((56, LANES), f32),
        in_specs=[hbm] * 5 + [pl.BlockSpec(memory_space=pltpu.SMEM)],
        out_specs=pl.BlockSpec(memory_space=pltpu.VMEM),
        scratch_shapes=[
            pltpu.VMEM((MB, RT, d), bf16),
            pltpu.VMEM((MB, RT, d), bf16),
            pltpu.VMEM((3, RT, d), bf16),
            pltpu.VMEM((SLOTS, 2, MB, RT, CC), bf16),
            pltpu.VMEM((2, SLOTS, MB, RT, CC), bf16),
            pltpu.VMEM((C, 3, RT, CC), bf16),
            pltpu.VMEM((3, HID, CC), bf16),
            pltpu.VMEM((SLOTS, 3 * TOK + 8, LANES), f32),
            pltpu.VMEM((SLOTS, 3 * TOK + 8, LANES), f32),
            pltpu.VMEM((SLOTS, 3, TOK, HID), bf16),
            pltpu.VMEM((Z, 208, LANES), bf16),
            pltpu.VMEM((Z, 208, LANES), bf16),
            pltpu.VMEM((YL * C, 24 * Z, LANES), bf16),
            pltpu.VMEM((Y, 24 * Z, LANES), bf16),
            pltpu.VMEM((YL * C, 32, LANES), f32),
            pltpu.VMEM((Y, 32, LANES), f32),
            pltpu.VMEM((Z, 24, LANES), f32),
            pltpu.VMEM((Z, 24, LANES), f32),
            dma((5,)),
            dma((SLOTS,)), dma((SLOTS,)),
            dma((9,)), dma((9,)),
            dma((SLOTS,)), dma((SLOTS,)),
            dma((SLOTS,)), dma((SLOTS,)),
            dma((Z,)), dma((Z,)),
            dma((Y,)), dma((Y,)),
            dma((Y,)), dma((Y,)),
            dma((Z,)), dma((Z,)),
        ],
        compiler_params=pltpu.CompilerParams(
            collective_id=0, has_side_effects=True, vmem_limit_bytes=40 * 1024 * 1024
        ),
        name="window_grads",
    )(acts, grad_out, w_gate.T, w_up.T, w_down, overflow)


def per_device(acts, grad_out, w_gate, w_up, w_down, overflow, step, master, moment1, moment2):
    n_dp = lax.axis_size("dp")
    micro = acts.shape[0]
    reduced = reduced_grads(acts, grad_out, w_gate, w_up, w_down, overflow)
    grad = reduced[:48].reshape(master.shape) / jnp.float32(micro * n_dp)
    count = reduced[48, 0] * jnp.float32(1.0 / (C * YL))
    keep = 1.0 - count / jnp.float32(micro * n_dp)
    new_moment1 = 0.9 * moment1 + 0.1 * grad
    new_moment2 = 0.95 * moment2 + 0.05 * grad * grad
    steps_f = step[0].astype(jnp.float32)
    corr1 = 1.0 - jnp.power(jnp.float32(0.9), steps_f)
    corr2 = 1.0 - jnp.power(jnp.float32(0.95), steps_f)
    direction = new_moment1 / corr1 / (jnp.sqrt(new_moment2 / corr2) + 1e-08)
    new_master = master - 0.01 * keep * (direction + 0.1 * master)
    return (new_master, new_moment1, new_moment2)


def solution(mesh):
    in_specs = (
        P(None, ("dp", "tensor"), None),
        P(None, ("dp", "tensor"), None),
        P(None, "tensor"),
        P(None, "tensor"),
        P("tensor", None),
        P("dp", None),
        P(),
        P(None, "tensor", "dp"),
        P(None, "tensor", "dp"),
        P(None, "tensor", "dp"),
    )
    out_specs = (P(None, "tensor", "dp"), P(None, "tensor", "dp"), P(None, "tensor", "dp"))
    return jax.shard_map(
        per_device, mesh=mesh, in_specs=in_specs, out_specs=out_specs, check_vma=False
    )
```

```python
import jax
import jax.numpy as jnp
from jax import lax
from jax.experimental import pallas as pl
from jax.experimental.pallas import tpu as pltpu
from jax.sharding import PartitionSpec as P

X, YH, YL, Z = 4, 2, 4, 8
Y = YH * YL
C = 2
MB, RT = 2, 16
TOK = MB * RT
SLOTS = 4 * C
LANES = 128
BLOCKS = (X // 2) * (Z // 2)
CC = BLOCKS * LANES
HID = 128
MESH = pl.DeviceIdType.MESH
NT = (((1,), (1,)), ((), ()))


def dev(y, z, x, c):
    return (lax.div(y, YL) * Z + z) * X + x, lax.rem(y, YL) * C + c


def kernel(
    acts_hbm, dy_hbm, wg_hbm, wu_hbm, wd_hbm, ovf_hbm, out, rate_out,
    ovf, acts_v, dy_v, w_v, sx, sd, bx, bd, sw, wb, pt, pd, rx, rd, ab, hb, sz, rz, sy, ry, s2y, r2y, s2z, r2z,
    n1, m2, m3, ld, xs, xr, ds, dr, ws, wr, ps, pr, qs, qr, as_, ar, hs, hr, zs, zr, ys, yr, y2s, y2r, z2s, z2r,
    n1s, n1r, n2s, n2r, n3s, n3r,
):
    dp, t = lax.axis_index("dp"), lax.axis_index("tensor")
    x = lax.rem(dp, X)
    z = lax.rem(lax.div(dp, X), Z)
    yh = lax.div(dp, X * Z)
    yl = lax.div(t, C)
    c = lax.rem(t, C)
    y = yh * YL + yl
    sib = 1 - c
    px, pz = lax.rem(x, 2), lax.rem(z, 2)
    me = (px * 2 + pz) * C + c
    kme = lax.div(z, 2) * (X // 2) + lax.div(x, 2)

    even_x, even_z = x + 1 - 2 * px, z + 1 - 2 * pz
    odd_x, odd_z = lax.rem(x + X - 1 + 2 * px, X), lax.rem(z + Z - 1 + 2 * pz, Z)

    def even(ex, ez, core):
        return dev(y, even_z if ez else z, even_x if ex else x, core)

    def odd(ex, ez, core):
        return dev(y, odd_z if ez else z, odd_x if ex else x, core)

    def across(bit, flip):
        return 1 - bit if flip else bit

    def slot(ex, ez, ec):
        return (across(px, ex) * 2 + across(pz, ez)) * C + across(c, ec)

    def number(ex, ez, ec):
        return (ex * 2 + ez) * C + ec

    others = [(1, 1, 0), (1, 1, 1), (1, 0, 0), (0, 1, 0), (1, 0, 1), (0, 1, 1), (0, 0, 1)]

    loads = [
        pltpu.make_async_copy(src, dst, ld.at[i])
        for i, (src, dst) in enumerate(
            [
                (wg_hbm, w_v.at[0]),
                (wu_hbm, w_v.at[1]),
                (wd_hbm, w_v.at[2]),
                (acts_hbm, acts_v),
                (dy_hbm, dy_v),
                (ovf_hbm, ovf),
            ]
        )
    ]
    for load in loads:
        load.start()

    barrier = pltpu.get_barrier_semaphore()
    friends = [even(ex, ez, across(c, ec)) for ex, ez, ec in others]
    friends += [odd(ex, ez, across(c, ec)) for ex, ez, ec in others if ex or ez]
    for step in range(1, Y):
        for dc in range(C):
            friends.append(dev(lax.rem(y + step, Y), z, x, across(c, dc)))

    def class_dev(k):
        return dev(y, lax.div(k, X // 2) * 2 + pz, lax.rem(k, X // 2) * 2 + px, c)

    for step in range(1, BLOCKS):
        friends.append(class_dev(lax.rem(kme + step, BLOCKS)))
    for friend in friends:
        pl.semaphore_signal(barrier, inc=1, device_id=friend, device_id_type=MESH)

    def columns(k, qx, qz, core):
        kz, kx = k // (X // 2), k % (X // 2)
        block = (core * Z + 2 * kz + qz) * X + 2 * kx + qx
        return pl.ds(pl.multiple_of(block * LANES, LANES), LANES)

    for load in loads[:3]:
        load.wait()
    for cp in range(C):
        for k in range(BLOCKS):
            sw[cp, :, :, k * LANES : (k + 1) * LANES] = w_v[:, :, columns(k, px, pz, cp)]
    pl.semaphore_wait(barrier, len(friends))

    sends = []

    def send(src, dst, send_sem, recv_sem, where):
        copy = pltpu.make_async_remote_copy(
            src_ref=src, dst_ref=dst, send_sem=send_sem, recv_sem=recv_sem, device_id=where, device_id_type=MESH
        )
        copy.start()
        return copy

    def arrived(dst, sem):
        pltpu.make_async_copy(dst, dst, sem).wait()

    same = c == yh

    def to_y(buf, slots, send_sems, recv_sems):
        for rel in range(1, YL * C):
            i = lax.rem(t + rel, YL * C)
            where = dev(c * YL + lax.div(i, C), z, x, lax.rem(i, C))
            sends.append(send(buf.at[i], slots.at[y], send_sems.at[rel], recv_sems.at[y], where))

        @pl.when(same)
        def _():
            slots[y] = buf[t]

        @pl.when(jnp.logical_not(same))
        def _():
            send(buf.at[t], slots.at[y], send_sems.at[0], recv_sems.at[y], dev(c * YL + yl, z, x, c))

    def from_y(buf, slots, send_sems, recv_sems):
        for rel in range(1, Y):
            arrived(slots.at[y], recv_sems.at[lax.rem(y + rel, Y)])

        @pl.when(jnp.logical_not(same))
        def _():
            arrived(slots.at[y], recv_sems.at[y])
            pltpu.make_async_copy(buf.at[t], buf.at[t], send_sems.at[0]).wait()

    def to_z(buf, slots, send_sems, recv_sems):
        for rel in range(1, BLOCKS):
            k = lax.rem(kme + rel, BLOCKS)
            sends.append(send(buf.at[k], slots.at[kme], send_sems.at[rel], recv_sems.at[kme], class_dev(k)))
        slots[kme] = buf[kme]

    def from_z(slots, recv_sems):
        for rel in range(1, BLOCKS):
            arrived(slots.at[kme], recv_sems.at[lax.rem(kme + rel, BLOCKS)])

    def added(slots, length):
        value = slots[0].astype(jnp.float32)
        for n in range(1, length):
            value = value + slots[n].astype(jnp.float32)
        return value

    rows = pl.ds(pl.multiple_of(t * RT, RT), RT)
    half = CC // 2
    one, two = slice(0, half), slice(half, CC)
    routes = [(Y - 1, one), (1, two), (Y - 1, two), (1, one)]
    for i, (hop, cols) in enumerate(routes):
        for cp in range(C):
            where = dev(lax.rem(y + hop, Y), z, x, cp)
            sends.append(send(sw.at[cp, :, :, cols], wb.at[:, rows, cols], ws.at[i * C + cp], wr.at[i * C + c], where))
    sends.append(send(sw.at[sib], wb.at[:, rows, :], ws.at[8], wr.at[8], dev(y, z, x, sib)))
    for load in loads[3:]:
        load.wait()
    for ex, ez, ec in others:
        n = number(ex, ez, ec)
        for k in range(BLOCKS):
            at = columns(k, across(px, ex), across(pz, ez), across(c, ec))
            sx[n, :, :, k * LANES : (k + 1) * LANES] = acts_v[:, :, at]
            sd[n, :, :, k * LANES : (k + 1) * LANES] = dy_v[:, :, at]
        sends.append(send(sx.at[n], bx.at[me], xs.at[n], xr.at[n], even(ex, ez, across(c, ec))))
        sends.append(send(sd.at[n], bd.at[me], ds.at[n], dr.at[n], odd(ex, ez, across(c, ec))))
    lost = (ovf[0, 0] + ovf[0, 1]).astype(jnp.float32)
    square = px * 2 + pz
    n1[square] = jnp.full((8, LANES), lost, jnp.float32)
    for n, (ex, ez) in enumerate([(1, 1), (1, 0), (0, 1)]):
        sends.append(send(n1.at[square], n1.at[square], n1s.at[n], n1r.at[n], even(ex, ez, c)))
    wb[:, rows, :] = sw[c]
    for k in range(BLOCKS):
        at = columns(k, px, pz, c)
        bx[me, :, :, k * LANES : (k + 1) * LANES] = acts_v[:, :, at]
        bd[me, :, :, k * LANES : (k + 1) * LANES] = dy_v[:, :, at]

    for i, (hop, cols) in enumerate(routes[:2]):
        for cp in range(C):
            arrived(wb.at[:, rows, cols], wr.at[i * C + cp])
        shard = pl.ds(pl.multiple_of(lax.rem(yl + YL - hop % YL, YL) * C * RT, C * RT), C * RT)
        where = dev(lax.rem(y + hop, Y), z, x, c)
        sends.append(send(wb.at[:, shard, cols], wb.at[:, shard, cols], ws.at[9 + i], wr.at[9 + i], where))

    pairs = [(1, 1), (1, 0), (0, 1), (0, 0)]
    for i, (hop, cols) in enumerate(routes[2:]):
        for cp in range(C):
            arrived(wb.at[:, rows, cols], wr.at[(2 + i) * C + cp])
    arrived(wb.at[:, rows, :], wr.at[8])
    for i, (hop, cols) in enumerate(routes[:2]):
        shard = pl.ds(0, C * RT)
        arrived(wb.at[:, shard, cols], wr.at[9 + i])
    for ex, ez in pairs:
        for ec in range(C):
            if ex or ez or ec:
                arrived(bx.at[me], xr.at[number(ex, ez, ec)])
        g = across(px, ex) * 2 + across(pz, ez)
        a = bx[pl.ds(g * C, C)].reshape(C * TOK, CC)
        gate_up = lax.dot_general(a, wb[0:2].reshape(2 * HID, CC), NT, preferred_element_type=jnp.float32)
        for cc in range(C):
            part = slice(cc * TOK, (cc + 1) * TOK)
            pt[g * C + cc, 0:TOK] = gate_up[part, :HID]
            pt[g * C + cc, TOK:] = gate_up[part, HID:]
        for ec in range(C):
            if ex or ez or ec:
                n, core = number(ex, ez, ec), across(c, ec)
                sends.append(send(pt.at[g * C + core], rx.at[me], ps.at[n], pr.at[n], even(ex, ez, core)))
    for ex, ez in pairs:
        for ec in range(C):
            if ex or ez or ec:
                arrived(bd.at[me], dr.at[number(ex, ez, ec)])
        g = across(px, ex) * 2 + across(pz, ez)
        d = bd[pl.ds(g * C, C)].reshape(C * TOK, CC)
        dh = lax.dot_general(d, wb[2], NT, preferred_element_type=jnp.float32)
        for cc in range(C):
            pd[g * C + cc] = dh[cc * TOK : (cc + 1) * TOK]
        for ec in range(C):
            if ex or ez or ec:
                n, core = number(ex, ez, ec), across(c, ec)
                sends.append(send(pd.at[g * C + core], rd.at[me], qs.at[n], qr.at[n], odd(ex, ez, core)))
    for n in range(3):
        arrived(n1.at[square], n1r.at[n])
    m2[kme] = added(n1, 4)
    for rel in range(1, BLOCKS):
        k = lax.rem(kme + rel, BLOCKS)
        sends.append(send(m2.at[kme], m2.at[kme], n2s.at[rel], n2r.at[kme], class_dev(k)))
    rx[me] = pt[me]
    rd[me] = pd[me]
    for n in range(1, SLOTS):
        arrived(rx.at[me], pr.at[n])
    total = rx[0]
    for n in range(1, SLOTS):
        total = total + rx[n]
    gate, up = total[:TOK], total[TOK:]
    sig = 1.0 / (1.0 + jnp.exp(-gate))
    silu = gate * sig
    first = lax.broadcasted_iota(jnp.int32, (TOK, HID), 0) < RT
    keep_rows = jnp.where(first, 1 - ovf[0, 0], 1 - ovf[0, 1]) > 0
    zero = jnp.zeros((TOK, HID), jnp.float32)
    hb[me] = jnp.where(keep_rows, silu * up, zero).astype(jnp.bfloat16)
    for ex, ez, ec in others:
        n = number(ex, ez, ec)
        sends.append(send(hb.at[me], hb.at[me], hs.at[n], hr.at[n], odd(ex, ez, across(c, ec))))
    for n in range(1, SLOTS):
        arrived(rd.at[me], qr.at[n])
    dh = rd[0]
    for n in range(1, SLOTS):
        dh = dh + rd[n]
    ab[me, 0] = jnp.where(keep_rows, dh * up * sig * (1.0 + gate * (1.0 - sig)), zero).astype(jnp.bfloat16)
    ab[me, 1] = jnp.where(keep_rows, dh * silu, zero).astype(jnp.bfloat16)
    for ex, ez, ec in others:
        n = number(ex, ez, ec)
        sends.append(send(ab.at[me], ab.at[me], as_.at[n], ar.at[n], even(ex, ez, across(c, ec))))
    from_z(m2, n2r)
    m3[yh] = added(m2, BLOCKS)
    sends.append(send(m3.at[yh], m3.at[yh], n3s, n3r, dev(lax.rem(y + YL, Y), z, x, c)))
    for n in range(1, SLOTS):
        arrived(hb.at[me], hr.at[n])
        arrived(ab.at[me], ar.at[n])

    lhs = [jnp.transpose(v.reshape(SLOTS * TOK, HID)) for v in (ab[:, 0], ab[:, 1], hb[...])]
    lhs_gu = jnp.concatenate(lhs[:2], axis=0)
    wide = 2 * LANES
    for zt in range(BLOCKS // 2):
        cols = slice(zt * wide, (zt + 1) * wide)
        acts_cols = bx[:, :, :, cols].reshape(SLOTS * TOK, wide)
        dy_cols = bd[:, :, :, cols].reshape(SLOTS * TOK, wide)
        gu = jnp.dot(lhs_gu, acts_cols, preferred_element_type=jnp.float32)
        dn = jnp.dot(lhs[2], dy_cols, preferred_element_type=jnp.float32)
        for k, block in enumerate([gu[:HID], gu[HID:], dn]):
            pair = [block[:, :LANES], block[:, LANES:]]
            for b in range(2):
                low = [pair[b][i * RT : i * RT + 8] for i in range(YL * C)]
                sz[zt * 2 + b, k * 64 : (k + 1) * 64] = jnp.concatenate(low, axis=0).astype(jnp.bfloat16)
            for i in range(YL * C):
                high = [p[i * RT + 8 : (i + 1) * RT] for p in pair]
                at = k * 8 * BLOCKS + zt * 16
                sy[i, at : at + 16] = jnp.concatenate(high, axis=0).astype(jnp.bfloat16)

    to_y(sy, ry, ys, yr)
    to_z(sz, rz, zs, zr)
    from_y(sy, ry, ys, yr)
    high = added(ry, Y)
    for k in range(BLOCKS):
        for m in range(3):
            at = m * 8 * BLOCKS + k * 8
            s2z[k, m * 8 : (m + 1) * 8] = high[at : at + 8]
    to_z(s2z, r2z, z2s, z2r)
    from_z(rz, zr)
    low = added(rz, BLOCKS)
    for i in range(YL * C):
        for m in range(3):
            s2y[i, m * 8 : (m + 1) * 8] = low[m * 64 + i * 8 : m * 64 + (i + 1) * 8]
    to_y(s2y, r2y, y2s, y2r)
    from_z(r2z, z2r)
    high = added(r2z, BLOCKS)
    from_y(s2y, r2y, y2s, y2r)
    low = added(r2y, Y)
    arrived(m3.at[yh], n3r)
    n_dp = lax.axis_size("dp")
    count = m3[0] + m3[1]
    rate = 0.01 * (1.0 - count / jnp.float32(MB * n_dp))
    for m in range(3):
        out[m, 0:8] = low[m * 8 : (m + 1) * 8] / jnp.float32(MB * n_dp)
        out[m, 8:16] = high[m * 8 : (m + 1) * 8] / jnp.float32(MB * n_dp)
        rate_out[m, 0:8] = rate
        rate_out[m, 8:16] = rate

    for copy in sends:
        copy.wait_send()


def per_device(acts, grad_out, w_gate, w_up, w_down, overflow, step, master, moment1, moment2):
    d = acts.shape[2]
    bf16, f32 = jnp.bfloat16, jnp.float32
    dma = pltpu.SemaphoreType.DMA
    grad, rate = pl.pallas_call(
        kernel,
        out_shape=(jax.ShapeDtypeStruct((3, RT, LANES), f32),) * 2,
        in_specs=[pl.BlockSpec(memory_space=pl.ANY)] * 6,
        out_specs=(pl.BlockSpec(memory_space=pltpu.VMEM),) * 2,
        scratch_shapes=[
            pltpu.SMEM((1, MB), jnp.int32),
            pltpu.VMEM((MB, RT, d), bf16),
            pltpu.VMEM((MB, RT, d), bf16),
            pltpu.VMEM((3, RT, d), bf16),
            pltpu.VMEM((SLOTS, MB, RT, CC), bf16),
            pltpu.VMEM((SLOTS, MB, RT, CC), bf16),
            pltpu.VMEM((SLOTS, MB, RT, CC), bf16),
            pltpu.VMEM((SLOTS, MB, RT, CC), bf16),
            pltpu.VMEM((C, 3, RT, CC), bf16),
            pltpu.VMEM((3, HID, CC), bf16),
            pltpu.VMEM((SLOTS, 2 * TOK, LANES), f32),
            pltpu.VMEM((SLOTS, TOK, LANES), f32),
            pltpu.VMEM((SLOTS, 2 * TOK, LANES), f32),
            pltpu.VMEM((SLOTS, TOK, LANES), f32),
            pltpu.VMEM((SLOTS, 2, TOK, HID), bf16),
            pltpu.VMEM((SLOTS, TOK, HID), bf16),
            pltpu.VMEM((BLOCKS, 192, LANES), bf16),
            pltpu.VMEM((BLOCKS, 192, LANES), bf16),
            pltpu.VMEM((YL * C, 24 * BLOCKS, LANES), bf16),
            pltpu.VMEM((Y, 24 * BLOCKS, LANES), bf16),
            pltpu.VMEM((YL * C, 24, LANES), f32),
            pltpu.VMEM((Y, 24, LANES), f32),
            pltpu.VMEM((BLOCKS, 24, LANES), f32),
            pltpu.VMEM((BLOCKS, 24, LANES), f32),
            pltpu.VMEM((4, 8, LANES), f32),
            pltpu.VMEM((BLOCKS, 8, LANES), f32),
            pltpu.VMEM((YH, 8, LANES), f32),
            dma((6,)),
            dma((SLOTS,)), dma((SLOTS,)),
            dma((SLOTS,)), dma((SLOTS,)),
            dma((11,)), dma((11,)),
            dma((SLOTS,)), dma((SLOTS,)),
            dma((SLOTS,)), dma((SLOTS,)),
            dma((SLOTS,)), dma((SLOTS,)),
            dma((SLOTS,)), dma((SLOTS,)),
            dma((BLOCKS,)), dma((BLOCKS,)),
            dma((Y,)), dma((Y,)),
            dma((Y,)), dma((Y,)),
            dma((BLOCKS,)), dma((BLOCKS,)),
            dma((3,)), dma((3,)),
            dma((BLOCKS,)), dma((BLOCKS,)),
            dma, dma,
        ],
        compiler_params=pltpu.CompilerParams(
            collective_id=0, has_side_effects=True, vmem_limit_bytes=63 * 1024 * 1024
        ),
        name="window_grads",
    )(acts, grad_out, w_gate.T, w_up.T, w_down, overflow)
    new_moment1 = 0.9 * moment1 + 0.1 * grad
    new_moment2 = 0.95 * moment2 + 0.05 * grad * grad
    steps_f = step[0].astype(f32)
    corr1 = 1.0 - jnp.power(f32(0.9), steps_f)
    corr2 = 1.0 - jnp.power(f32(0.95), steps_f)
    direction = new_moment1 / corr1 / (jnp.sqrt(new_moment2 / corr2) + 1e-08)
    new_master = master - rate * (direction + 0.1 * master)
    return (new_master, new_moment1, new_moment2)


def solution(mesh):
    in_specs = (
        P(None, ("dp", "tensor"), None),
        P(None, ("dp", "tensor"), None),
        P(None, "tensor"),
        P(None, "tensor"),
        P("tensor", None),
        P("dp", None),
        P(),
        P(None, "tensor", "dp"),
        P(None, "tensor", "dp"),
        P(None, "tensor", "dp"),
    )
    out_specs = (P(None, "tensor", "dp"), P(None, "tensor", "dp"), P(None, "tensor", "dp"))
    return jax.shard_map(
        per_device, mesh=mesh, in_specs=in_specs, out_specs=out_specs, check_vma=False
    )
```

```python
import jax
import jax.numpy as jnp
from jax import lax
from jax.experimental import pallas as pl
from jax.experimental.pallas import tpu as pltpu
from jax.sharding import PartitionSpec as P

X, YH, YL, Z = 4, 2, 4, 8
Y = YH * YL
C = 2
MB, RT = 2, 16
TOK = MB * RT
SLOTS = 4 * C
LANES = 128
BLOCKS = (X // 2) * (Z // 2)
CC = BLOCKS * LANES
HID = 128
LOW = (8, 8, 8)
MESH = pl.DeviceIdType.MESH
NT = (((1,), (1,)), ((), ()))


def dev(y, z, x, c):
    return (lax.div(y, YL) * Z + z) * X + x, lax.rem(y, YL) * C + c


def kernel(
    acts_hbm, dy_hbm, wg_hbm, wu_hbm, wd_hbm, ovf_hbm, out, rate_out,
    ovf, acts_v, dy_v, w_v, sx, sd, bx, bd, sw, wb, pt, pd, rx, rd, ab, hb, sz, rz, sy, ry, s2y, r2y, s2z, r2z,
    n1, m2, m3, ld, xs, xr, ds, dr, ws, wr, ps, pr, qs, qr, as_, ar, hs, hr, zs, zr, ys, yr, y2s, y2r, z2s, z2r,
    n1s, n1r, n2s, n2r, n3s, n3r,
):
    dp, t = lax.axis_index("dp"), lax.axis_index("tensor")
    x = lax.rem(dp, X)
    z = lax.rem(lax.div(dp, X), Z)
    yh = lax.div(dp, X * Z)
    yl = lax.div(t, C)
    c = lax.rem(t, C)
    y = yh * YL + yl
    sib = 1 - c
    px, pz = lax.rem(x, 2), lax.rem(z, 2)
    me = (px * 2 + pz) * C + c
    kme = lax.div(z, 2) * (X // 2) + lax.div(x, 2)

    even_x, even_z = x + 1 - 2 * px, z + 1 - 2 * pz
    odd_x, odd_z = lax.rem(x + X - 1 + 2 * px, X), lax.rem(z + Z - 1 + 2 * pz, Z)

    def even(ex, ez, core):
        return dev(y, even_z if ez else z, even_x if ex else x, core)

    def odd(ex, ez, core):
        return dev(y, odd_z if ez else z, odd_x if ex else x, core)

    def across(bit, flip):
        return 1 - bit if flip else bit

    def slot(ex, ez, ec):
        return (across(px, ex) * 2 + across(pz, ez)) * C + across(c, ec)

    def number(ex, ez, ec):
        return (ex * 2 + ez) * C + ec

    others = [(1, 1, 0), (1, 1, 1), (1, 0, 0), (0, 1, 0), (1, 0, 1), (0, 1, 1), (0, 0, 1)]

    loads = [
        pltpu.make_async_copy(src, dst, ld.at[i])
        for i, (src, dst) in enumerate(
            [
                (wg_hbm, w_v.at[0]),
                (wu_hbm, w_v.at[1]),
                (wd_hbm, w_v.at[2]),
                (acts_hbm, acts_v),
                (dy_hbm, dy_v),
                (ovf_hbm, ovf),
            ]
        )
    ]
    for load in loads:
        load.start()

    barrier = pltpu.get_barrier_semaphore()
    friends = [even(ex, ez, across(c, ec)) for ex, ez, ec in others]
    friends += [odd(ex, ez, across(c, ec)) for ex, ez, ec in others if ex or ez]
    for step in range(1, Y):
        for dc in range(C):
            friends.append(dev(lax.rem(y + step, Y), z, x, across(c, dc)))

    def class_dev(k):
        return dev(y, lax.div(k, X // 2) * 2 + pz, lax.rem(k, X // 2) * 2 + px, c)

    for friend in friends:
        pl.semaphore_signal(barrier, inc=1, device_id=friend, device_id_type=MESH)

    def columns(k, qx, qz, core):
        kz, kx = k // (X // 2), k % (X // 2)
        block = (core * Z + 2 * kz + qz) * X + 2 * kx + qx
        return pl.ds(pl.multiple_of(block * LANES, LANES), LANES)

    for load in loads[:3]:
        load.wait()
    for cp in range(C):
        for k in range(BLOCKS):
            sw[cp, :, :, k * LANES : (k + 1) * LANES] = w_v[:, :, columns(k, px, pz, cp)]
    pl.semaphore_wait(barrier, len(friends))

    sends = []

    def send(src, dst, send_sem, recv_sem, where):
        copy = pltpu.make_async_remote_copy(
            src_ref=src, dst_ref=dst, send_sem=send_sem, recv_sem=recv_sem, device_id=where, device_id_type=MESH
        )
        copy.start()
        return copy

    def arrived(dst, sem):
        pltpu.make_async_copy(dst, dst, sem).wait()

    same = c == yh

    def to_y(buf, slots, send_sems, recv_sems):
        for rel in range(1, YL * C):
            i = lax.rem(t + rel, YL * C)
            where = dev(c * YL + lax.div(i, C), z, x, lax.rem(i, C))
            sends.append(send(buf.at[i], slots.at[y], send_sems.at[rel], recv_sems.at[y], where))

        @pl.when(same)
        def _():
            slots[y] = buf[t]

        @pl.when(jnp.logical_not(same))
        def _():
            send(buf.at[t], slots.at[y], send_sems.at[0], recv_sems.at[y], dev(c * YL + yl, z, x, c))

    def from_y(buf, slots, send_sems, recv_sems):
        for rel in range(1, Y):
            arrived(slots.at[y], recv_sems.at[lax.rem(y + rel, Y)])

        @pl.when(jnp.logical_not(same))
        def _():
            arrived(slots.at[y], recv_sems.at[y])
            pltpu.make_async_copy(buf.at[t], buf.at[t], send_sems.at[0]).wait()

    def to_z(buf, slots, send_sems, recv_sems):
        for rel in range(1, BLOCKS):
            k = lax.rem(kme + rel, BLOCKS)
            sends.append(send(buf.at[k], slots.at[kme], send_sems.at[rel], recv_sems.at[kme], class_dev(k)))
        slots[kme] = buf[kme]

    def from_z(slots, recv_sems):
        for rel in range(1, BLOCKS):
            arrived(slots.at[kme], recv_sems.at[lax.rem(kme + rel, BLOCKS)])

    def added(slots, length):
        value = slots[0].astype(jnp.float32)
        for n in range(1, length):
            value = value + slots[n].astype(jnp.float32)
        return value

    rows = pl.ds(pl.multiple_of(t * RT, RT), RT)
    half = CC // 2
    one, two = slice(0, half), slice(half, CC)
    routes = [(Y - 1, one), (1, two), (Y - 1, two), (1, one)]
    for i, (hop, cols) in enumerate(routes):
        for cp in range(C):
            where = dev(lax.rem(y + hop, Y), z, x, cp)
            sends.append(send(sw.at[cp, :, :, cols], wb.at[:, rows, cols], ws.at[i * C + cp], wr.at[i * C + c], where))
    sends.append(send(sw.at[sib], wb.at[:, rows, :], ws.at[8], wr.at[8], dev(y, z, x, sib)))
    for load in loads[3:]:
        load.wait()
    for ex, ez, ec in others:
        n = number(ex, ez, ec)
        for k in range(BLOCKS):
            at = columns(k, across(px, ex), across(pz, ez), across(c, ec))
            sx[n, :, :, k * LANES : (k + 1) * LANES] = acts_v[:, :, at]
            sd[n, :, :, k * LANES : (k + 1) * LANES] = dy_v[:, :, at]
        sends.append(send(sx.at[n], bx.at[me], xs.at[n], xr.at[n], even(ex, ez, across(c, ec))))
        sends.append(send(sd.at[n], bd.at[me], ds.at[n], dr.at[n], odd(ex, ez, across(c, ec))))
    lost = (ovf[0, 0] + ovf[0, 1]).astype(jnp.float32)
    m3[yh] = jnp.full((8, LANES), lost, jnp.float32)
    sends.append(send(m3.at[yh], m3.at[yh], n3s, n3r, dev(lax.rem(y + YL, Y), z, x, c)))
    wb[:, rows, :] = sw[c]
    for k in range(BLOCKS):
        at = columns(k, px, pz, c)
        bx[me, :, :, k * LANES : (k + 1) * LANES] = acts_v[:, :, at]
        bd[me, :, :, k * LANES : (k + 1) * LANES] = dy_v[:, :, at]

    for i, (hop, cols) in enumerate(routes[:2]):
        for cp in range(C):
            arrived(wb.at[:, rows, cols], wr.at[i * C + cp])
        shard = pl.ds(pl.multiple_of(lax.rem(yl + YL - hop % YL, YL) * C * RT, C * RT), C * RT)
        where = dev(lax.rem(y + hop, Y), z, x, c)
        sends.append(send(wb.at[:, shard, cols], wb.at[:, shard, cols], ws.at[9 + i], wr.at[9 + i], where))

    square = px * 2 + pz
    arrived(m3.at[yh], n3r)
    n1[square] = m3[0] + m3[1]
    for n, (ex, ez) in enumerate([(1, 1), (1, 0), (0, 1)]):
        sends.append(send(n1.at[square], n1.at[square], n1s.at[n], n1r.at[n], even(ex, ez, c)))

    pairs = [(1, 1), (1, 0), (0, 1), (0, 0)]
    for i, (hop, cols) in enumerate(routes[2:]):
        for cp in range(C):
            arrived(wb.at[:, rows, cols], wr.at[(2 + i) * C + cp])
    arrived(wb.at[:, rows, :], wr.at[8])
    for i, (hop, cols) in enumerate(routes[:2]):
        shard = pl.ds(0, C * RT)
        arrived(wb.at[:, shard, cols], wr.at[9 + i])
    for ex, ez in pairs:
        for ec in range(C):
            if ex or ez or ec:
                arrived(bx.at[me], xr.at[number(ex, ez, ec)])
        g = across(px, ex) * 2 + across(pz, ez)
        a = bx[pl.ds(g * C, C)].reshape(C * TOK, CC)
        gate_up = lax.dot_general(a, wb[0:2].reshape(2 * HID, CC), NT, preferred_element_type=jnp.float32)
        for cc in range(C):
            part = slice(cc * TOK, (cc + 1) * TOK)
            pt[g * C + cc, 0:TOK] = gate_up[part, :HID]
            pt[g * C + cc, TOK:] = gate_up[part, HID:]
        for ec in range(C):
            if ex or ez or ec:
                n, core = number(ex, ez, ec), across(c, ec)
                sends.append(send(pt.at[g * C + core], rx.at[me], ps.at[n], pr.at[n], even(ex, ez, core)))
    for ex, ez in pairs:
        for ec in range(C):
            if ex or ez or ec:
                arrived(bd.at[me], dr.at[number(ex, ez, ec)])
        g = across(px, ex) * 2 + across(pz, ez)
        d = bd[pl.ds(g * C, C)].reshape(C * TOK, CC)
        dh = lax.dot_general(d, wb[2], NT, preferred_element_type=jnp.float32)
        for cc in range(C):
            pd[g * C + cc] = dh[cc * TOK : (cc + 1) * TOK]
        for ec in range(C):
            if ex or ez or ec:
                n, core = number(ex, ez, ec), across(c, ec)
                sends.append(send(pd.at[g * C + core], rd.at[me], qs.at[n], qr.at[n], odd(ex, ez, core)))
    rx[me] = pt[me]
    rd[me] = pd[me]
    for n in range(1, SLOTS):
        arrived(rx.at[me], pr.at[n])
    total = rx[0]
    for n in range(1, SLOTS):
        total = total + rx[n]
    gate, up = total[:TOK], total[TOK:]
    sig = 1.0 / (1.0 + jnp.exp(-gate))
    silu = gate * sig
    first = lax.broadcasted_iota(jnp.int32, (TOK, HID), 0) < RT
    keep_rows = jnp.where(first, 1 - ovf[0, 0], 1 - ovf[0, 1]) > 0
    zero = jnp.zeros((TOK, HID), jnp.float32)
    hb[me] = jnp.where(keep_rows, silu * up, zero).astype(jnp.bfloat16)
    for ex, ez, ec in others:
        n = number(ex, ez, ec)
        sends.append(send(hb.at[me], hb.at[me], hs.at[n], hr.at[n], odd(ex, ez, across(c, ec))))
    for n in range(1, SLOTS):
        arrived(rd.at[me], qr.at[n])
    dh = rd[0]
    for n in range(1, SLOTS):
        dh = dh + rd[n]
    ab[me, 0] = jnp.where(keep_rows, dh * up * sig * (1.0 + gate * (1.0 - sig)), zero).astype(jnp.bfloat16)
    ab[me, 1] = jnp.where(keep_rows, dh * silu, zero).astype(jnp.bfloat16)
    for ex, ez, ec in others:
        n = number(ex, ez, ec)
        sends.append(send(ab.at[me], ab.at[me], as_.at[n], ar.at[n], even(ex, ez, across(c, ec))))
    for n in range(1, SLOTS):
        arrived(hb.at[me], hr.at[n])
        arrived(ab.at[me], ar.at[n])

    lhs = [jnp.transpose(v.reshape(SLOTS * TOK, HID)) for v in (ab[:, 0], ab[:, 1], hb[...])]
    lhs_gu = jnp.concatenate(lhs[:2], axis=0)
    wide = 2 * LANES
    for zt in range(BLOCKS // 2):
        cols = slice(zt * wide, (zt + 1) * wide)
        acts_cols = bx[:, :, :, cols].reshape(SLOTS * TOK, wide)
        dy_cols = bd[:, :, :, cols].reshape(SLOTS * TOK, wide)
        gu = jnp.dot(lhs_gu, acts_cols, preferred_element_type=jnp.float32)
        dn = jnp.dot(lhs[2], dy_cols, preferred_element_type=jnp.float32)
        for k, block in enumerate([gu[:HID], gu[HID:], dn]):
            pair = [block[:, :LANES], block[:, LANES:]]
            n_low, n_high = LOW[k], RT - LOW[k]
            for b in range(2):
                low = [pair[b][i * RT : i * RT + n_low] for i in range(YL * C)]
                at = sum(LOW[:k]) * YL * C
                sz[zt * 2 + b, at : at + n_low * YL * C] = jnp.concatenate(low, axis=0).astype(jnp.bfloat16)
            for i in range(YL * C if n_high else 0):
                high = [p[i * RT + n_low : (i + 1) * RT] for p in pair]
                at = (k * RT - sum(LOW[:k])) * BLOCKS + zt * 2 * n_high
                sy[i, at : at + 2 * n_high] = jnp.concatenate(high, axis=0).astype(jnp.bfloat16)

    to_y(sy, ry, ys, yr)
    to_z(sz, rz, zs, zr)
    for n in range(3):
        arrived(n1.at[square], n1r.at[n])
    m2[kme] = added(n1, 4)
    for rel in range(1, BLOCKS):
        k = lax.rem(kme + rel, BLOCKS)
        sends.append(send(m2.at[kme], m2.at[kme], n2s.at[rel], n2r.at[kme], class_dev(k)))
    from_y(sy, ry, ys, yr)
    high = added(ry, Y)
    for k in range(BLOCKS):
        for m in range(3):
            n_high, to = RT - LOW[m], m * RT - sum(LOW[:m])
            if n_high:
                at = to * BLOCKS + k * n_high
                s2z[k, to : to + n_high] = high[at : at + n_high]
    to_z(s2z, r2z, z2s, z2r)
    from_z(rz, zr)
    low = added(rz, BLOCKS)
    for i in range(YL * C):
        for m in range(3):
            n_low, to = LOW[m], sum(LOW[:m])
            at = to * YL * C + i * n_low
            s2y[i, to : to + n_low] = low[at : at + n_low]
    to_y(s2y, r2y, y2s, y2r)
    from_z(r2z, z2r)
    high = added(r2z, BLOCKS)
    from_y(s2y, r2y, y2s, y2r)
    low = added(r2y, Y)
    from_z(m2, n2r)
    n_dp = lax.axis_size("dp")
    count = added(m2, BLOCKS)
    rate = 0.01 * (1.0 - count / jnp.float32(MB * n_dp))
    for m in range(3):
        n_low, at = LOW[m], sum(LOW[:m])
        out[m, 0:n_low] = low[at : at + n_low] / jnp.float32(MB * n_dp)
        if n_low < RT:
            at = m * RT - at
            out[m, n_low:RT] = high[at : at + RT - n_low] / jnp.float32(MB * n_dp)
        rate_out[m, 0:8] = rate
        rate_out[m, 8:16] = rate

    for copy in sends:
        copy.wait_send()


def per_device(acts, grad_out, w_gate, w_up, w_down, overflow, step, master, moment1, moment2):
    d = acts.shape[2]
    bf16, f32 = jnp.bfloat16, jnp.float32
    dma = pltpu.SemaphoreType.DMA
    grad, rate = pl.pallas_call(
        kernel,
        out_shape=(jax.ShapeDtypeStruct((3, RT, LANES), f32),) * 2,
        in_specs=[pl.BlockSpec(memory_space=pl.ANY)] * 6,
        out_specs=(pl.BlockSpec(memory_space=pltpu.VMEM),) * 2,
        scratch_shapes=[
            pltpu.SMEM((1, MB), jnp.int32),
            pltpu.VMEM((MB, RT, d), bf16),
            pltpu.VMEM((MB, RT, d), bf16),
            pltpu.VMEM((3, RT, d), bf16),
            pltpu.VMEM((SLOTS, MB, RT, CC), bf16),
            pltpu.VMEM((SLOTS, MB, RT, CC), bf16),
            pltpu.VMEM((SLOTS, MB, RT, CC), bf16),
            pltpu.VMEM((SLOTS, MB, RT, CC), bf16),
            pltpu.VMEM((C, 3, RT, CC), bf16),
            pltpu.VMEM((3, HID, CC), bf16),
            pltpu.VMEM((SLOTS, 2 * TOK, LANES), f32),
            pltpu.VMEM((SLOTS, TOK, LANES), f32),
            pltpu.VMEM((SLOTS, 2 * TOK, LANES), f32),
            pltpu.VMEM((SLOTS, TOK, LANES), f32),
            pltpu.VMEM((SLOTS, 2, TOK, HID), bf16),
            pltpu.VMEM((SLOTS, TOK, HID), bf16),
            pltpu.VMEM((BLOCKS, sum(LOW) * YL * C, LANES), bf16),
            pltpu.VMEM((BLOCKS, sum(LOW) * YL * C, LANES), bf16),
            pltpu.VMEM((YL * C, (3 * RT - sum(LOW)) * BLOCKS, LANES), bf16),
            pltpu.VMEM((Y, (3 * RT - sum(LOW)) * BLOCKS, LANES), bf16),
            pltpu.VMEM((YL * C, sum(LOW), LANES), f32),
            pltpu.VMEM((Y, sum(LOW), LANES), f32),
            pltpu.VMEM((BLOCKS, 3 * RT - sum(LOW), LANES), f32),
            pltpu.VMEM((BLOCKS, 3 * RT - sum(LOW), LANES), f32),
            pltpu.VMEM((4, 8, LANES), f32),
            pltpu.VMEM((BLOCKS, 8, LANES), f32),
            pltpu.VMEM((YH, 8, LANES), f32),
            dma((6,)),
            dma((SLOTS,)), dma((SLOTS,)),
            dma((SLOTS,)), dma((SLOTS,)),
            dma((11,)), dma((11,)),
            dma((SLOTS,)), dma((SLOTS,)),
            dma((SLOTS,)), dma((SLOTS,)),
            dma((SLOTS,)), dma((SLOTS,)),
            dma((SLOTS,)), dma((SLOTS,)),
            dma((BLOCKS,)), dma((BLOCKS,)),
            dma((Y,)), dma((Y,)),
            dma((Y,)), dma((Y,)),
            dma((BLOCKS,)), dma((BLOCKS,)),
            dma((3,)), dma((3,)),
            dma((BLOCKS,)), dma((BLOCKS,)),
            dma, dma,
        ],
        compiler_params=pltpu.CompilerParams(
            collective_id=0, has_side_effects=True, vmem_limit_bytes=63 * 1024 * 1024
        ),
        name="window_grads",
    )(acts, grad_out, w_gate.T, w_up.T, w_down, overflow)
    new_moment1 = 0.9 * moment1 + 0.1 * grad
    new_moment2 = 0.95 * moment2 + 0.05 * grad * grad
    steps_f = step[0].astype(f32)
    corr1 = 1.0 - jnp.power(f32(0.9), steps_f)
    corr2 = 1.0 - jnp.power(f32(0.95), steps_f)
    direction = new_moment1 / corr1 / (jnp.sqrt(new_moment2 / corr2) + 1e-08)
    new_master = master - rate * (direction + 0.1 * master)
    return (new_master, new_moment1, new_moment2)


def solution(mesh):
    in_specs = (
        P(None, ("dp", "tensor"), None),
        P(None, ("dp", "tensor"), None),
        P(None, "tensor"),
        P(None, "tensor"),
        P("tensor", None),
        P("dp", None),
        P(),
        P(None, "tensor", "dp"),
        P(None, "tensor", "dp"),
        P(None, "tensor", "dp"),
    )
    out_specs = (P(None, "tensor", "dp"), P(None, "tensor", "dp"), P(None, "tensor", "dp"))
    return jax.shard_map(
        per_device, mesh=mesh, in_specs=in_specs, out_specs=out_specs, check_vma=False
    )
```

```python
import jax
import jax.numpy as jnp
from jax import lax
from jax.experimental import pallas as pl
from jax.experimental.pallas import tpu as pltpu
from jax.sharding import PartitionSpec as P

X, YH, YL, Z = 4, 2, 4, 8
Y = YH * YL
C = 2
MB, RT = 2, 16
TOK = MB * RT
SLOTS = 4 * C
LANES = 128
BLOCKS = (X // 2) * (Z // 2)
CC = BLOCKS * LANES
HID = 128
LOW = 8
MESH = pl.DeviceIdType.MESH
NT = (((1,), (1,)), ((), ()))


def dev(y, z, x, c):
    return (lax.div(y, YL) * Z + z) * X + x, lax.rem(y, YL) * C + c


def kernel(
    acts_hbm, dy_hbm, wg_hbm, wu_hbm, wd_hbm, ovf_hbm, out, rate_out,
    ovf, acts_v, dy_v, w_v, sx, sd, bx, bd, sw, wb, pt, pd, rx, rd, ab, hb, sz, rz, sy, ry, szd, rzd, syd, ryd, s2y, r2y, s2z, r2z,
    n1, m2, m3, ld, xs, xr, ds, dr, ws, wr, ps, pr, qs, qr, as_, ar, hs, hr, zs, zr, ys, yr, zds, zdr, yds, ydr, y2s, y2r, z2s, z2r,
    n1s, n1r, n2s, n2r, n3s, n3r,
):
    dp, t = lax.axis_index("dp"), lax.axis_index("tensor")
    x = lax.rem(dp, X)
    z = lax.rem(lax.div(dp, X), Z)
    yh = lax.div(dp, X * Z)
    yl = lax.div(t, C)
    c = lax.rem(t, C)
    y = yh * YL + yl
    sib = 1 - c
    px, pz = lax.rem(x, 2), lax.rem(z, 2)
    me = (px * 2 + pz) * C + c
    kme = lax.div(z, 2) * (X // 2) + lax.div(x, 2)

    even_x, even_z = x + 1 - 2 * px, z + 1 - 2 * pz
    odd_x, odd_z = lax.rem(x + X - 1 + 2 * px, X), lax.rem(z + Z - 1 + 2 * pz, Z)

    def even(ex, ez, core):
        return dev(y, even_z if ez else z, even_x if ex else x, core)

    def odd(ex, ez, core):
        return dev(y, odd_z if ez else z, odd_x if ex else x, core)

    def across(bit, flip):
        return 1 - bit if flip else bit

    def slot(ex, ez, ec):
        return (across(px, ex) * 2 + across(pz, ez)) * C + across(c, ec)

    def number(ex, ez, ec):
        return (ex * 2 + ez) * C + ec

    others = [(1, 1, 0), (1, 1, 1), (1, 0, 0), (0, 1, 0), (1, 0, 1), (0, 1, 1), (0, 0, 1)]

    loads = [
        pltpu.make_async_copy(src, dst, ld.at[i])
        for i, (src, dst) in enumerate(
            [
                (wg_hbm, w_v.at[0]),
                (wu_hbm, w_v.at[1]),
                (wd_hbm, w_v.at[2]),
                (acts_hbm, acts_v),
                (dy_hbm, dy_v),
                (ovf_hbm, ovf),
            ]
        )
    ]
    for load in loads:
        load.start()

    barrier = pltpu.get_barrier_semaphore()
    friends = [even(ex, ez, across(c, ec)) for ex, ez, ec in others]
    friends += [odd(ex, ez, across(c, ec)) for ex, ez, ec in others if ex or ez]
    for step in range(1, Y):
        for dc in range(C):
            friends.append(dev(lax.rem(y + step, Y), z, x, across(c, dc)))

    def class_dev(k):
        return dev(y, lax.div(k, X // 2) * 2 + pz, lax.rem(k, X // 2) * 2 + px, c)

    for friend in friends:
        pl.semaphore_signal(barrier, inc=1, device_id=friend, device_id_type=MESH)

    def columns(k, qx, qz, core):
        kz, kx = k // (X // 2), k % (X // 2)
        block = (core * Z + 2 * kz + qz) * X + 2 * kx + qx
        return pl.ds(pl.multiple_of(block * LANES, LANES), LANES)

    for load in loads[:3]:
        load.wait()
    for cp in range(C):
        for k in range(BLOCKS):
            sw[cp, :, :, k * LANES : (k + 1) * LANES] = w_v[:, :, columns(k, px, pz, cp)]
    pl.semaphore_wait(barrier, len(friends))

    sends = []

    def send(src, dst, send_sem, recv_sem, where):
        copy = pltpu.make_async_remote_copy(
            src_ref=src, dst_ref=dst, send_sem=send_sem, recv_sem=recv_sem, device_id=where, device_id_type=MESH
        )
        copy.start()
        return copy

    def arrived(dst, sem):
        pltpu.make_async_copy(dst, dst, sem).wait()

    same = c == yh

    def to_y(buf, slots, send_sems, recv_sems):
        for rel in range(1, YL * C):
            i = lax.rem(t + rel, YL * C)
            where = dev(c * YL + lax.div(i, C), z, x, lax.rem(i, C))
            sends.append(send(buf.at[i], slots.at[y], send_sems.at[rel], recv_sems.at[y], where))

        @pl.when(same)
        def _():
            slots[y] = buf[t]

        @pl.when(jnp.logical_not(same))
        def _():
            send(buf.at[t], slots.at[y], send_sems.at[0], recv_sems.at[y], dev(c * YL + yl, z, x, c))

    def from_y(buf, slots, send_sems, recv_sems):
        for rel in range(1, Y):
            arrived(slots.at[y], recv_sems.at[lax.rem(y + rel, Y)])

        @pl.when(jnp.logical_not(same))
        def _():
            arrived(slots.at[y], recv_sems.at[y])
            pltpu.make_async_copy(buf.at[t], buf.at[t], send_sems.at[0]).wait()

    near = [(0, 1), (1, 0), (1, 1), (3, 0), (3, 1)]
    far = [(2, 0), (2, 1)]

    def to_z(buf, slots, send_sems, recv_sems, steps):
        for kz, kx in steps:
            k = lax.rem(lax.div(z, 2) + kz, Z // 2) * 2 + across(lax.div(x, 2), kx)
            sends.append(send(buf.at[k], slots.at[kme], send_sems.at[kz * 2 + kx], recv_sems.at[kme], class_dev(k)))

    def from_z(slots, recv_sems):
        for rel in range(1, BLOCKS):
            arrived(slots.at[kme], recv_sems.at[lax.rem(kme + rel, BLOCKS)])

    def added(slots, length):
        value = slots[0].astype(jnp.float32)
        for n in range(1, length):
            value = value + slots[n].astype(jnp.float32)
        return value

    rows = pl.ds(pl.multiple_of(t * RT, RT), RT)
    half = CC // 2
    one, two = slice(0, half), slice(half, CC)
    routes = [(Y - 1, one), (1, two), (Y - 1, two), (1, one)]
    for i, (hop, cols) in enumerate(routes):
        for cp in range(C):
            where = dev(lax.rem(y + hop, Y), z, x, cp)
            sends.append(send(sw.at[cp, :, :, cols], wb.at[:, rows, cols], ws.at[i * C + cp], wr.at[i * C + c], where))
    sends.append(send(sw.at[sib], wb.at[:, rows, :], ws.at[8], wr.at[8], dev(y, z, x, sib)))
    for load in loads[3:]:
        load.wait()
    for ex, ez, ec in others:
        n = number(ex, ez, ec)
        for k in range(BLOCKS):
            at = columns(k, across(px, ex), across(pz, ez), across(c, ec))
            sx[n, :, :, k * LANES : (k + 1) * LANES] = acts_v[:, :, at]
            sd[n, :, :, k * LANES : (k + 1) * LANES] = dy_v[:, :, at]
        sends.append(send(sx.at[n], bx.at[me], xs.at[n], xr.at[n], even(ex, ez, across(c, ec))))
        sends.append(send(sd.at[n], bd.at[me], ds.at[n], dr.at[n], odd(ex, ez, across(c, ec))))
    lost = (ovf[0, 0] + ovf[0, 1]).astype(jnp.float32)
    m3[yh] = jnp.full((8, LANES), lost, jnp.float32)
    sends.append(send(m3.at[yh], m3.at[yh], n3s, n3r, dev(lax.rem(y + YL, Y), z, x, c)))
    wb[:, rows, :] = sw[c]
    for k in range(BLOCKS):
        at = columns(k, px, pz, c)
        bx[me, :, :, k * LANES : (k + 1) * LANES] = acts_v[:, :, at]
        bd[me, :, :, k * LANES : (k + 1) * LANES] = dy_v[:, :, at]

    for i, (hop, cols) in enumerate(routes[:2]):
        for cp in range(C):
            arrived(wb.at[:, rows, cols], wr.at[i * C + cp])
        shard = pl.ds(pl.multiple_of(lax.rem(yl + YL - hop % YL, YL) * C * RT, C * RT), C * RT)
        where = dev(lax.rem(y + hop, Y), z, x, c)
        sends.append(send(wb.at[:, shard, cols], wb.at[:, shard, cols], ws.at[9 + i], wr.at[9 + i], where))

    square = px * 2 + pz
    arrived(m3.at[yh], n3r)
    n1[square] = m3[0] + m3[1]
    for n, (ex, ez) in enumerate([(1, 1), (1, 0), (0, 1)]):
        sends.append(send(n1.at[square], n1.at[square], n1s.at[n], n1r.at[n], even(ex, ez, c)))

    pairs = [(1, 1), (1, 0), (0, 1), (0, 0)]
    for i, (hop, cols) in enumerate(routes[2:]):
        for cp in range(C):
            arrived(wb.at[:, rows, cols], wr.at[(2 + i) * C + cp])
    arrived(wb.at[:, rows, :], wr.at[8])
    for i, (hop, cols) in enumerate(routes[:2]):
        shard = pl.ds(0, C * RT)
        arrived(wb.at[:, shard, cols], wr.at[9 + i])
    for ex, ez in pairs:
        for ec in range(C):
            if ex or ez or ec:
                arrived(bx.at[me], xr.at[number(ex, ez, ec)])
        g = across(px, ex) * 2 + across(pz, ez)
        a = bx[pl.ds(g * C, C)].reshape(C * TOK, CC)
        gate_up = lax.dot_general(a, wb[0:2].reshape(2 * HID, CC), NT, preferred_element_type=jnp.float32)
        for cc in range(C):
            part = slice(cc * TOK, (cc + 1) * TOK)
            pt[g * C + cc, 0:TOK] = gate_up[part, :HID]
            pt[g * C + cc, TOK:] = gate_up[part, HID:]
        for ec in range(C):
            if ex or ez or ec:
                n, core = number(ex, ez, ec), across(c, ec)
                sends.append(send(pt.at[g * C + core], rx.at[me], ps.at[n], pr.at[n], even(ex, ez, core)))
    for ex, ez in pairs:
        for ec in range(C):
            if ex or ez or ec:
                arrived(bd.at[me], dr.at[number(ex, ez, ec)])
        g = across(px, ex) * 2 + across(pz, ez)
        d = bd[pl.ds(g * C, C)].reshape(C * TOK, CC)
        dh = lax.dot_general(d, wb[2], NT, preferred_element_type=jnp.float32)
        for cc in range(C):
            pd[g * C + cc] = dh[cc * TOK : (cc + 1) * TOK]
        for ec in range(C):
            if ex or ez or ec:
                n, core = number(ex, ez, ec), across(c, ec)
                sends.append(send(pd.at[g * C + core], rd.at[me], qs.at[n], qr.at[n], odd(ex, ez, core)))
    rx[me] = pt[me]
    rd[me] = pd[me]
    for n in range(1, SLOTS):
        arrived(rx.at[me], pr.at[n])
    total = rx[0]
    for n in range(1, SLOTS):
        total = total + rx[n]
    gate, up = total[:TOK], total[TOK:]
    sig = 1.0 / (1.0 + jnp.exp(-gate))
    silu = gate * sig
    first = lax.broadcasted_iota(jnp.int32, (TOK, HID), 0) < RT
    keep_rows = jnp.where(first, 1 - ovf[0, 0], 1 - ovf[0, 1]) > 0
    zero = jnp.zeros((TOK, HID), jnp.float32)
    hb[me] = jnp.where(keep_rows, silu * up, zero).astype(jnp.bfloat16)
    for ex, ez, ec in others:
        n = number(ex, ez, ec)
        sends.append(send(hb.at[me], hb.at[me], hs.at[n], hr.at[n], odd(ex, ez, across(c, ec))))
    for n in range(1, SLOTS):
        arrived(rd.at[me], qr.at[n])
    dh = rd[0]
    for n in range(1, SLOTS):
        dh = dh + rd[n]
    ab[me, 0] = jnp.where(keep_rows, dh * up * sig * (1.0 + gate * (1.0 - sig)), zero).astype(jnp.bfloat16)
    ab[me, 1] = jnp.where(keep_rows, dh * silu, zero).astype(jnp.bfloat16)
    for ex, ez, ec in others:
        n = number(ex, ez, ec)
        sends.append(send(ab.at[me], ab.at[me], as_.at[n], ar.at[n], even(ex, ez, across(c, ec))))
    def products(lhs, tokens, low_buf, high_buf):
        wide = 2 * LANES
        for zt in range(BLOCKS // 2):
            cols = slice(zt * wide, (zt + 1) * wide)
            rhs = tokens[:, :, :, cols].reshape(SLOTS * TOK, wide)
            summed = jnp.dot(lhs, rhs, preferred_element_type=jnp.float32)
            for k in range(lhs.shape[0] // HID):
                block = summed[k * HID : (k + 1) * HID]
                pair = [block[:, :LANES], block[:, LANES:]]
                at = k * LOW * YL * C
                for b in range(2):
                    low = [pair[b][i * RT : i * RT + LOW] for i in range(YL * C)]
                    low_buf[zt * 2 + b, at : at + LOW * YL * C] = jnp.concatenate(low, axis=0).astype(jnp.bfloat16)
                at = k * 8 * BLOCKS + zt * 16
                for i in range(YL * C):
                    high = [p[i * RT + LOW : (i + 1) * RT] for p in pair]
                    high_buf[i, at : at + 16] = jnp.concatenate(high, axis=0).astype(jnp.bfloat16)

    for n in range(1, SLOTS):
        arrived(hb.at[me], hr.at[n])
    products(jnp.transpose(hb[...].reshape(SLOTS * TOK, HID)), bd, szd, syd)
    to_y(syd, ryd, yds, ydr)
    to_z(szd, rzd, zds, zdr, near)
    for n in range(1, SLOTS):
        arrived(ab.at[me], ar.at[n])
    to_z(szd, rzd, zds, zdr, far)
    rzd[kme] = szd[kme]
    lhs = [jnp.transpose(ab[:, k].reshape(SLOTS * TOK, HID)) for k in range(2)]
    products(jnp.concatenate(lhs, axis=0), bx, sz, sy)
    to_y(sy, ry, ys, yr)
    to_z(sz, rz, zs, zr, near + far)
    rz[kme] = sz[kme]
    for n in range(3):
        arrived(n1.at[square], n1r.at[n])
    m2[kme] = added(n1, 4)
    for rel in range(1, BLOCKS):
        k = lax.rem(kme + rel, BLOCKS)
        sends.append(send(m2.at[kme], m2.at[kme], n2s.at[rel], n2r.at[kme], class_dev(k)))
    from_y(syd, ryd, yds, ydr)
    from_y(sy, ry, ys, yr)
    high = (added(ry, Y), added(ryd, Y))
    for k in range(BLOCKS):
        for m in range(3):
            at = m % 2 * 8 * BLOCKS + k * 8
            s2z[k, m * 8 : (m + 1) * 8] = high[m // 2][at : at + 8]
    to_z(s2z, r2z, z2s, z2r, near + far)
    r2z[kme] = s2z[kme]
    from_z(rzd, zdr)
    from_z(rz, zr)
    low = (added(rz, BLOCKS), added(rzd, BLOCKS))
    for i in range(YL * C):
        for m in range(3):
            at = m % 2 * LOW * YL * C + i * LOW
            s2y[i, m * LOW : (m + 1) * LOW] = low[m // 2][at : at + LOW]
    to_y(s2y, r2y, y2s, y2r)
    from_z(r2z, z2r)
    high = added(r2z, BLOCKS)
    from_y(s2y, r2y, y2s, y2r)
    low = added(r2y, Y)
    from_z(m2, n2r)
    n_dp = lax.axis_size("dp")
    count = added(m2, BLOCKS)
    rate = 0.01 * (1.0 - count / jnp.float32(MB * n_dp))
    for m in range(3):
        out[m, 0:8] = low[m * 8 : (m + 1) * 8] / jnp.float32(MB * n_dp)
        out[m, 8:16] = high[m * 8 : (m + 1) * 8] / jnp.float32(MB * n_dp)
        rate_out[m, 0:8] = rate
        rate_out[m, 8:16] = rate

    for copy in sends:
        copy.wait_send()


def per_device(acts, grad_out, w_gate, w_up, w_down, overflow, step, master, moment1, moment2):
    d = acts.shape[2]
    bf16, f32 = jnp.bfloat16, jnp.float32
    dma = pltpu.SemaphoreType.DMA
    grad, rate = pl.pallas_call(
        kernel,
        out_shape=(jax.ShapeDtypeStruct((3, RT, LANES), f32),) * 2,
        in_specs=[pl.BlockSpec(memory_space=pl.ANY)] * 6,
        out_specs=(pl.BlockSpec(memory_space=pltpu.VMEM),) * 2,
        scratch_shapes=[
            pltpu.SMEM((1, MB), jnp.int32),
            pltpu.VMEM((MB, RT, d), bf16),
            pltpu.VMEM((MB, RT, d), bf16),
            pltpu.VMEM((3, RT, d), bf16),
            pltpu.VMEM((SLOTS, MB, RT, CC), bf16),
            pltpu.VMEM((SLOTS, MB, RT, CC), bf16),
            pltpu.VMEM((SLOTS, MB, RT, CC), bf16),
            pltpu.VMEM((SLOTS, MB, RT, CC), bf16),
            pltpu.VMEM((C, 3, RT, CC), bf16),
            pltpu.VMEM((3, HID, CC), bf16),
            pltpu.VMEM((SLOTS, 2 * TOK, LANES), f32),
            pltpu.VMEM((SLOTS, TOK, LANES), f32),
            pltpu.VMEM((SLOTS, 2 * TOK, LANES), f32),
            pltpu.VMEM((SLOTS, TOK, LANES), f32),
            pltpu.VMEM((SLOTS, 2, TOK, HID), bf16),
            pltpu.VMEM((SLOTS, TOK, HID), bf16),
            pltpu.VMEM((BLOCKS, 2 * LOW * YL * C, LANES), bf16),
            pltpu.VMEM((BLOCKS, 2 * LOW * YL * C, LANES), bf16),
            pltpu.VMEM((YL * C, 2 * 8 * BLOCKS, LANES), bf16),
            pltpu.VMEM((Y, 2 * 8 * BLOCKS, LANES), bf16),
            pltpu.VMEM((BLOCKS, LOW * YL * C, LANES), bf16),
            pltpu.VMEM((BLOCKS, LOW * YL * C, LANES), bf16),
            pltpu.VMEM((YL * C, 8 * BLOCKS, LANES), bf16),
            pltpu.VMEM((Y, 8 * BLOCKS, LANES), bf16),
            pltpu.VMEM((YL * C, 3 * LOW, LANES), f32),
            pltpu.VMEM((Y, 3 * LOW, LANES), f32),
            pltpu.VMEM((BLOCKS, 24, LANES), f32),
            pltpu.VMEM((BLOCKS, 24, LANES), f32),
            pltpu.VMEM((4, 8, LANES), f32),
            pltpu.VMEM((BLOCKS, 8, LANES), f32),
            pltpu.VMEM((YH, 8, LANES), f32),
            dma((6,)),
            dma((SLOTS,)), dma((SLOTS,)),
            dma((SLOTS,)), dma((SLOTS,)),
            dma((11,)), dma((11,)),
            dma((SLOTS,)), dma((SLOTS,)),
            dma((SLOTS,)), dma((SLOTS,)),
            dma((SLOTS,)), dma((SLOTS,)),
            dma((SLOTS,)), dma((SLOTS,)),
            dma((BLOCKS,)), dma((BLOCKS,)),
            dma((Y,)), dma((Y,)),
            dma((BLOCKS,)), dma((BLOCKS,)),
            dma((Y,)), dma((Y,)),
            dma((Y,)), dma((Y,)),
            dma((BLOCKS,)), dma((BLOCKS,)),
            dma((3,)), dma((3,)),
            dma((BLOCKS,)), dma((BLOCKS,)),
            dma, dma,
        ],
        compiler_params=pltpu.CompilerParams(
            collective_id=0, has_side_effects=True, vmem_limit_bytes=63 * 1024 * 1024
        ),
        name="window_grads",
    )(acts, grad_out, w_gate.T, w_up.T, w_down, overflow)
    new_moment1 = 0.9 * moment1 + 0.1 * grad
    new_moment2 = 0.95 * moment2 + 0.05 * grad * grad
    steps_f = step[0].astype(f32)
    corr1 = 1.0 - jnp.power(f32(0.9), steps_f)
    corr2 = 1.0 - jnp.power(f32(0.95), steps_f)
    direction = new_moment1 / corr1 / (jnp.sqrt(new_moment2 / corr2) + 1e-08)
    new_master = master - rate * (direction + 0.1 * master)
    return (new_master, new_moment1, new_moment2)


def solution(mesh):
    in_specs = (
        P(None, ("dp", "tensor"), None),
        P(None, ("dp", "tensor"), None),
        P(None, "tensor"),
        P(None, "tensor"),
        P("tensor", None),
        P("dp", None),
        P(),
        P(None, "tensor", "dp"),
        P(None, "tensor", "dp"),
        P(None, "tensor", "dp"),
    )
    out_specs = (P(None, "tensor", "dp"), P(None, "tensor", "dp"), P(None, "tensor", "dp"))
    return jax.shard_map(
        per_device, mesh=mesh, in_specs=in_specs, out_specs=out_specs, check_vma=False
    )
```

```python
import jax
import jax.numpy as jnp
from jax import lax
from jax.experimental import pallas as pl
from jax.experimental.pallas import tpu as pltpu
from jax.sharding import PartitionSpec as P

X, YH, YL, Z = 4, 2, 4, 8
Y = YH * YL
C = 2
MB, RT = 2, 16
TOK = MB * RT
SLOTS = 4 * C
LANES = 128
BLOCKS = (X // 2) * (Z // 2)
CC = BLOCKS * LANES
HID = 128
LOW = 8
MESH = pl.DeviceIdType.MESH
NT = (((1,), (1,)), ((), ()))


def dev(y, z, x, c):
    return (lax.div(y, YL) * Z + z) * X + x, lax.rem(y, YL) * C + c


def kernel(
    acts_hbm, dy_hbm, wg_hbm, wu_hbm, wd_hbm, ovf_hbm, out, rate_out,
    ovf, acts_v, dy_v, w_v, sx, sd, bx, bd, sw, wb, pt, pd, rx, rd, ab, hb, sz, rz, sy, ry, szd, rzd, syd, ryd, s2y, r2y, s2z, r2z,
    n1, m2, m3, ld, xs, xr, ds, dr, ws, wr, vs, vr, ps, pr, qs, qr, as_, ar, hs, hr, zs, zr, ys, yr, zds, zdr, yds, ydr, y2s, y2r, z2s, z2r,
    n1s, n1r, n2s, n2r, n3s, n3r,
):
    dp, t = lax.axis_index("dp"), lax.axis_index("tensor")
    x = lax.rem(dp, X)
    z = lax.rem(lax.div(dp, X), Z)
    yh = lax.div(dp, X * Z)
    yl = lax.div(t, C)
    c = lax.rem(t, C)
    y = yh * YL + yl
    sib = 1 - c
    px, pz = lax.rem(x, 2), lax.rem(z, 2)
    me = (px * 2 + pz) * C + c
    kme = lax.div(z, 2) * (X // 2) + lax.div(x, 2)

    even_x, even_z = x + 1 - 2 * px, z + 1 - 2 * pz
    odd_x, odd_z = lax.rem(x + X - 1 + 2 * px, X), lax.rem(z + Z - 1 + 2 * pz, Z)

    def even(ex, ez, core):
        return dev(y, even_z if ez else z, even_x if ex else x, core)

    def odd(ex, ez, core):
        return dev(y, odd_z if ez else z, odd_x if ex else x, core)

    def across(bit, flip):
        return 1 - bit if flip else bit

    def slot(ex, ez, ec):
        return (across(px, ex) * 2 + across(pz, ez)) * C + across(c, ec)

    def number(ex, ez, ec):
        return (ex * 2 + ez) * C + ec

    others = [(1, 1, 0), (1, 1, 1), (1, 0, 0), (0, 1, 0), (1, 0, 1), (0, 1, 1), (0, 0, 1)]

    loads = [
        pltpu.make_async_copy(src, dst, ld.at[i])
        for i, (src, dst) in enumerate(
            [
                (wg_hbm, w_v.at[0]),
                (wu_hbm, w_v.at[1]),
                (wd_hbm, w_v.at[2]),
                (acts_hbm, acts_v),
                (dy_hbm, dy_v),
                (ovf_hbm, ovf),
            ]
        )
    ]
    for load in loads:
        load.start()

    barrier = pltpu.get_barrier_semaphore()
    friends = [even(ex, ez, across(c, ec)) for ex, ez, ec in others]
    friends += [odd(ex, ez, across(c, ec)) for ex, ez, ec in others if ex or ez]
    for step in range(1, Y):
        for dc in range(C):
            friends.append(dev(lax.rem(y + step, Y), z, x, across(c, dc)))

    def class_dev(k):
        return dev(y, lax.div(k, X // 2) * 2 + pz, lax.rem(k, X // 2) * 2 + px, c)

    for friend in friends:
        pl.semaphore_signal(barrier, inc=1, device_id=friend, device_id_type=MESH)

    def columns(k, qx, qz, core):
        kz, kx = k // (X // 2), k % (X // 2)
        block = (core * Z + 2 * kz + qz) * X + 2 * kx + qx
        return pl.ds(pl.multiple_of(block * LANES, LANES), LANES)

    for load in loads[:3]:
        load.wait()
    for cp in range(C):
        for k in range(BLOCKS):
            sw[cp, :, :, k * LANES : (k + 1) * LANES] = w_v[:, :, columns(k, px, pz, cp)]
    pl.semaphore_wait(barrier, len(friends))

    sends = []

    def send(src, dst, send_sem, recv_sem, where):
        copy = pltpu.make_async_remote_copy(
            src_ref=src, dst_ref=dst, send_sem=send_sem, recv_sem=recv_sem, device_id=where, device_id_type=MESH
        )
        copy.start()
        return copy

    def arrived(dst, sem):
        pltpu.make_async_copy(dst, dst, sem).wait()

    same = c == yh

    def to_y(buf, slots, send_sems, recv_sems):
        for rel in range(1, YL * C):
            i = lax.rem(t + rel, YL * C)
            where = dev(c * YL + lax.div(i, C), z, x, lax.rem(i, C))
            sends.append(send(buf.at[i], slots.at[y], send_sems.at[rel], recv_sems.at[y], where))

        @pl.when(same)
        def _():
            slots[y] = buf[t]

        @pl.when(jnp.logical_not(same))
        def _():
            send(buf.at[t], slots.at[y], send_sems.at[0], recv_sems.at[y], dev(c * YL + yl, z, x, c))

    def from_y(buf, slots, send_sems, recv_sems):
        for rel in range(1, Y):
            arrived(slots.at[y], recv_sems.at[lax.rem(y + rel, Y)])

        @pl.when(jnp.logical_not(same))
        def _():
            arrived(slots.at[y], recv_sems.at[y])
            pltpu.make_async_copy(buf.at[t], buf.at[t], send_sems.at[0]).wait()

    near = [(0, 1), (1, 0), (1, 1), (3, 0), (3, 1)]
    far = [(2, 0), (2, 1)]

    def to_z(buf, slots, send_sems, recv_sems, steps):
        for kz, kx in steps:
            k = lax.rem(lax.div(z, 2) + kz, Z // 2) * 2 + across(lax.div(x, 2), kx)
            sends.append(send(buf.at[k], slots.at[kme], send_sems.at[kz * 2 + kx], recv_sems.at[kme], class_dev(k)))

    def from_z(slots, recv_sems):
        for rel in range(1, BLOCKS):
            arrived(slots.at[kme], recv_sems.at[lax.rem(kme + rel, BLOCKS)])

    def added(slots, length):
        value = slots[0].astype(jnp.float32)
        for n in range(1, length):
            value = value + slots[n].astype(jnp.float32)
        return value

    rows = pl.ds(pl.multiple_of(t * RT, RT), RT)
    half = CC // 2
    one, two = slice(0, half), slice(half, CC)
    up, down = slice(0, 2), slice(2, 3)
    routes = [(Y - 1, one), (1, two), (Y - 1, two), (1, one)]
    for i, (hop, cols) in enumerate(routes):
        for cp in range(C):
            where = dev(lax.rem(y + hop, Y), z, x, cp)
            n, to = i * C + cp, i * C + c
            sends.append(send(sw.at[cp, up, :, cols], wb.at[up, rows, cols], ws.at[n], wr.at[to], where))
    sends.append(send(sw.at[sib, up], wb.at[up, rows, :], ws.at[8], wr.at[8], dev(y, z, x, sib)))
    for load in loads[3:]:
        load.wait()
    for ex, ez, ec in others:
        n = number(ex, ez, ec)
        for k in range(BLOCKS):
            at = columns(k, across(px, ex), across(pz, ez), across(c, ec))
            sx[n, :, :, k * LANES : (k + 1) * LANES] = acts_v[:, :, at]
            sd[n, :, :, k * LANES : (k + 1) * LANES] = dy_v[:, :, at]
        sends.append(send(sx.at[n], bx.at[me], xs.at[n], xr.at[n], even(ex, ez, across(c, ec))))
        sends.append(send(sd.at[n], bd.at[me], ds.at[n], dr.at[n], odd(ex, ez, across(c, ec))))
    lost = (ovf[0, 0] + ovf[0, 1]).astype(jnp.float32)
    m3[yh] = jnp.full((8, LANES), lost, jnp.float32)
    sends.append(send(m3.at[yh], m3.at[yh], n3s, n3r, dev(lax.rem(y + YL, Y), z, x, c)))
    wb[:, rows, :] = sw[c]
    for k in range(BLOCKS):
        at = columns(k, px, pz, c)
        bx[me, :, :, k * LANES : (k + 1) * LANES] = acts_v[:, :, at]
        bd[me, :, :, k * LANES : (k + 1) * LANES] = dy_v[:, :, at]

    for i, (hop, cols) in enumerate(routes[:2]):
        for cp in range(C):
            arrived(wb.at[up, rows, cols], wr.at[i * C + cp])
        shard = pl.ds(pl.multiple_of(lax.rem(yl + YL - hop % YL, YL) * C * RT, C * RT), C * RT)
        where = dev(lax.rem(y + hop, Y), z, x, c)
        sends.append(send(wb.at[up, shard, cols], wb.at[up, shard, cols], ws.at[9 + i], wr.at[9 + i], where))
    hops = [(2, one), (Y - 2, two), (1, slice(0, CC)), (Y - 1, slice(0, CC))]
    for i, (hop, cols) in enumerate(hops):
        for cp in range(C):
            n, to, where = i * C + cp, i * C + c, dev(lax.rem(y + hop, Y), z, x, cp)
            sends.append(send(sw.at[cp, down, :, cols], wb.at[down, rows, cols], vs.at[n], vr.at[to], where))
    sends.append(send(sw.at[sib, down], wb.at[down, rows, :], vs.at[8], vr.at[8], dev(y, z, x, sib)))

    square = px * 2 + pz
    arrived(m3.at[yh], n3r)
    n1[square] = m3[0] + m3[1]
    for n, (ex, ez) in enumerate([(1, 1), (1, 0), (0, 1)]):
        sends.append(send(n1.at[square], n1.at[square], n1s.at[n], n1r.at[n], even(ex, ez, c)))

    pairs = [(1, 1), (1, 0), (0, 1), (0, 0)]
    for i, (hop, cols) in enumerate(routes[2:]):
        for cp in range(C):
            arrived(wb.at[up, rows, cols], wr.at[(2 + i) * C + cp])
    arrived(wb.at[up, rows, :], wr.at[8])
    for i, (hop, cols) in enumerate(routes[:2]):
        shard = pl.ds(0, C * RT)
        arrived(wb.at[up, shard, cols], wr.at[9 + i])
    for ex, ez in pairs:
        for ec in range(C):
            if ex or ez or ec:
                arrived(bx.at[me], xr.at[number(ex, ez, ec)])
        g = across(px, ex) * 2 + across(pz, ez)
        a = bx[pl.ds(g * C, C)].reshape(C * TOK, CC)
        gate_up = lax.dot_general(a, wb[0:2].reshape(2 * HID, CC), NT, preferred_element_type=jnp.float32)
        for cc in range(C):
            part = slice(cc * TOK, (cc + 1) * TOK)
            pt[g * C + cc, 0:TOK] = gate_up[part, :HID]
            pt[g * C + cc, TOK:] = gate_up[part, HID:]
        for ec in range(C):
            if ex or ez or ec:
                n, core = number(ex, ez, ec), across(c, ec)
                sends.append(send(pt.at[g * C + core], rx.at[me], ps.at[n], pr.at[n], even(ex, ez, core)))
    for i, (hop, cols) in enumerate(hops):
        for cp in range(C):
            arrived(wb.at[down, rows, cols], vr.at[i * C + cp])
    arrived(wb.at[down, rows, :], vr.at[8])
    for ex, ez in pairs:
        for ec in range(C):
            if ex or ez or ec:
                arrived(bd.at[me], dr.at[number(ex, ez, ec)])
        g = across(px, ex) * 2 + across(pz, ez)
        d = bd[pl.ds(g * C, C)].reshape(C * TOK, CC)
        dh = lax.dot_general(d, wb[2], NT, preferred_element_type=jnp.float32)
        for cc in range(C):
            pd[g * C + cc] = dh[cc * TOK : (cc + 1) * TOK]
        for ec in range(C):
            if ex or ez or ec:
                n, core = number(ex, ez, ec), across(c, ec)
                sends.append(send(pd.at[g * C + core], rd.at[me], qs.at[n], qr.at[n], odd(ex, ez, core)))
    rx[me] = pt[me]
    rd[me] = pd[me]
    for n in range(1, SLOTS):
        arrived(rx.at[me], pr.at[n])
    total = rx[0]
    for n in range(1, SLOTS):
        total = total + rx[n]
    gate, up = total[:TOK], total[TOK:]
    sig = 1.0 / (1.0 + jnp.exp(-gate))
    silu = gate * sig
    first = lax.broadcasted_iota(jnp.int32, (TOK, HID), 0) < RT
    keep_rows = jnp.where(first, 1 - ovf[0, 0], 1 - ovf[0, 1]) > 0
    zero = jnp.zeros((TOK, HID), jnp.float32)
    hb[me] = jnp.where(keep_rows, silu * up, zero).astype(jnp.bfloat16)
    for ex, ez, ec in others:
        n = number(ex, ez, ec)
        sends.append(send(hb.at[me], hb.at[me], hs.at[n], hr.at[n], odd(ex, ez, across(c, ec))))
    for n in range(1, SLOTS):
        arrived(rd.at[me], qr.at[n])
    dh = rd[0]
    for n in range(1, SLOTS):
        dh = dh + rd[n]
    ab[me, 0] = jnp.where(keep_rows, dh * up * sig * (1.0 + gate * (1.0 - sig)), zero).astype(jnp.bfloat16)
    ab[me, 1] = jnp.where(keep_rows, dh * silu, zero).astype(jnp.bfloat16)
    for ex, ez, ec in others:
        n = number(ex, ez, ec)
        sends.append(send(ab.at[me], ab.at[me], as_.at[n], ar.at[n], even(ex, ez, across(c, ec))))
    def products(lhs, tokens, low_buf, high_buf):
        wide = 2 * LANES
        for zt in range(BLOCKS // 2):
            cols = slice(zt * wide, (zt + 1) * wide)
            rhs = tokens[:, :, :, cols].reshape(SLOTS * TOK, wide)
            summed = jnp.dot(lhs, rhs, preferred_element_type=jnp.float32)
            for k in range(lhs.shape[0] // HID):
                block = summed[k * HID : (k + 1) * HID]
                pair = [block[:, :LANES], block[:, LANES:]]
                at = k * LOW * YL * C
                for b in range(2):
                    low = [pair[b][i * RT : i * RT + LOW] for i in range(YL * C)]
                    low_buf[zt * 2 + b, at : at + LOW * YL * C] = jnp.concatenate(low, axis=0).astype(jnp.bfloat16)
                at = k * 8 * BLOCKS + zt * 16
                for i in range(YL * C):
                    high = [p[i * RT + LOW : (i + 1) * RT] for p in pair]
                    high_buf[i, at : at + 16] = jnp.concatenate(high, axis=0).astype(jnp.bfloat16)

    for n in range(1, SLOTS):
        arrived(hb.at[me], hr.at[n])
    products(jnp.transpose(hb[...].reshape(SLOTS * TOK, HID)), bd, szd, syd)
    to_y(syd, ryd, yds, ydr)
    to_z(szd, rzd, zds, zdr, near)
    for n in range(1, SLOTS):
        arrived(ab.at[me], ar.at[n])
    to_z(szd, rzd, zds, zdr, far)
    rzd[kme] = szd[kme]
    lhs = [jnp.transpose(ab[:, k].reshape(SLOTS * TOK, HID)) for k in range(2)]
    products(jnp.concatenate(lhs, axis=0), bx, sz, sy)
    to_y(sy, ry, ys, yr)
    to_z(sz, rz, zs, zr, near + far)
    rz[kme] = sz[kme]
    for n in range(3):
        arrived(n1.at[square], n1r.at[n])
    m2[kme] = added(n1, 4)
    for rel in range(1, BLOCKS):
        k = lax.rem(kme + rel, BLOCKS)
        sends.append(send(m2.at[kme], m2.at[kme], n2s.at[rel], n2r.at[kme], class_dev(k)))
    from_y(syd, ryd, yds, ydr)
    from_y(sy, ry, ys, yr)
    high = (added(ry, Y), added(ryd, Y))
    for k in range(BLOCKS):
        for m in range(3):
            at = m % 2 * 8 * BLOCKS + k * 8
            s2z[k, m * 8 : (m + 1) * 8] = high[m // 2][at : at + 8]
    to_z(s2z, r2z, z2s, z2r, near + far)
    r2z[kme] = s2z[kme]
    from_z(rzd, zdr)
    from_z(rz, zr)
    low = (added(rz, BLOCKS), added(rzd, BLOCKS))
    for i in range(YL * C):
        for m in range(3):
            at = m % 2 * LOW * YL * C + i * LOW
            s2y[i, m * LOW : (m + 1) * LOW] = low[m // 2][at : at + LOW]
    to_y(s2y, r2y, y2s, y2r)
    from_z(r2z, z2r)
    high = added(r2z, BLOCKS)
    from_y(s2y, r2y, y2s, y2r)
    low = added(r2y, Y)
    from_z(m2, n2r)
    n_dp = lax.axis_size("dp")
    count = added(m2, BLOCKS)
    rate = 0.01 * (1.0 - count / jnp.float32(MB * n_dp))
    for m in range(3):
        out[m, 0:8] = low[m * 8 : (m + 1) * 8] / jnp.float32(MB * n_dp)
        out[m, 8:16] = high[m * 8 : (m + 1) * 8] / jnp.float32(MB * n_dp)
        rate_out[m, 0:8] = rate
        rate_out[m, 8:16] = rate

    for copy in sends:
        copy.wait_send()


def per_device(acts, grad_out, w_gate, w_up, w_down, overflow, step, master, moment1, moment2):
    d = acts.shape[2]
    bf16, f32 = jnp.bfloat16, jnp.float32
    dma = pltpu.SemaphoreType.DMA
    grad, rate = pl.pallas_call(
        kernel,
        out_shape=(jax.ShapeDtypeStruct((3, RT, LANES), f32),) * 2,
        in_specs=[pl.BlockSpec(memory_space=pl.ANY)] * 6,
        out_specs=(pl.BlockSpec(memory_space=pltpu.VMEM),) * 2,
        scratch_shapes=[
            pltpu.SMEM((1, MB), jnp.int32),
            pltpu.VMEM((MB, RT, d), bf16),
            pltpu.VMEM((MB, RT, d), bf16),
            pltpu.VMEM((3, RT, d), bf16),
            pltpu.VMEM((SLOTS, MB, RT, CC), bf16),
            pltpu.VMEM((SLOTS, MB, RT, CC), bf16),
            pltpu.VMEM((SLOTS, MB, RT, CC), bf16),
            pltpu.VMEM((SLOTS, MB, RT, CC), bf16),
            pltpu.VMEM((C, 3, RT, CC), bf16),
            pltpu.VMEM((3, HID, CC), bf16),
            pltpu.VMEM((SLOTS, 2 * TOK, LANES), f32),
            pltpu.VMEM((SLOTS, TOK, LANES), f32),
            pltpu.VMEM((SLOTS, 2 * TOK, LANES), f32),
            pltpu.VMEM((SLOTS, TOK, LANES), f32),
            pltpu.VMEM((SLOTS, 2, TOK, HID), bf16),
            pltpu.VMEM((SLOTS, TOK, HID), bf16),
            pltpu.VMEM((BLOCKS, 2 * LOW * YL * C, LANES), bf16),
            pltpu.VMEM((BLOCKS, 2 * LOW * YL * C, LANES), bf16),
            pltpu.VMEM((YL * C, 2 * 8 * BLOCKS, LANES), bf16),
            pltpu.VMEM((Y, 2 * 8 * BLOCKS, LANES), bf16),
            pltpu.VMEM((BLOCKS, LOW * YL * C, LANES), bf16),
            pltpu.VMEM((BLOCKS, LOW * YL * C, LANES), bf16),
            pltpu.VMEM((YL * C, 8 * BLOCKS, LANES), bf16),
            pltpu.VMEM((Y, 8 * BLOCKS, LANES), bf16),
            pltpu.VMEM((YL * C, 3 * LOW, LANES), f32),
            pltpu.VMEM((Y, 3 * LOW, LANES), f32),
            pltpu.VMEM((BLOCKS, 24, LANES), f32),
            pltpu.VMEM((BLOCKS, 24, LANES), f32),
            pltpu.VMEM((4, 8, LANES), f32),
            pltpu.VMEM((BLOCKS, 8, LANES), f32),
            pltpu.VMEM((YH, 8, LANES), f32),
            dma((6,)),
            dma((SLOTS,)), dma((SLOTS,)),
            dma((SLOTS,)), dma((SLOTS,)),
            dma((11,)), dma((11,)),
            dma((9,)), dma((9,)),
            dma((SLOTS,)), dma((SLOTS,)),
            dma((SLOTS,)), dma((SLOTS,)),
            dma((SLOTS,)), dma((SLOTS,)),
            dma((SLOTS,)), dma((SLOTS,)),
            dma((BLOCKS,)), dma((BLOCKS,)),
            dma((Y,)), dma((Y,)),
            dma((BLOCKS,)), dma((BLOCKS,)),
            dma((Y,)), dma((Y,)),
            dma((Y,)), dma((Y,)),
            dma((BLOCKS,)), dma((BLOCKS,)),
            dma((3,)), dma((3,)),
            dma((BLOCKS,)), dma((BLOCKS,)),
            dma, dma,
        ],
        compiler_params=pltpu.CompilerParams(
            collective_id=0, has_side_effects=True, vmem_limit_bytes=63 * 1024 * 1024
        ),
        name="window_grads",
    )(acts, grad_out, w_gate.T, w_up.T, w_down, overflow)
    new_moment1 = 0.9 * moment1 + 0.1 * grad
    new_moment2 = 0.95 * moment2 + 0.05 * grad * grad
    steps_f = step[0].astype(f32)
    corr1 = 1.0 - jnp.power(f32(0.9), steps_f)
    corr2 = 1.0 - jnp.power(f32(0.95), steps_f)
    direction = new_moment1 / corr1 / (jnp.sqrt(new_moment2 / corr2) + 1e-08)
    new_master = master - rate * (direction + 0.1 * master)
    return (new_master, new_moment1, new_moment2)


def solution(mesh):
    in_specs = (
        P(None, ("dp", "tensor"), None),
        P(None, ("dp", "tensor"), None),
        P(None, "tensor"),
        P(None, "tensor"),
        P("tensor", None),
        P("dp", None),
        P(),
        P(None, "tensor", "dp"),
        P(None, "tensor", "dp"),
        P(None, "tensor", "dp"),
    )
    out_specs = (P(None, "tensor", "dp"), P(None, "tensor", "dp"), P(None, "tensor", "dp"))
    return jax.shard_map(
        per_device, mesh=mesh, in_specs=in_specs, out_specs=out_specs, check_vma=False
    )
```

```python
import jax
import jax.numpy as jnp
from jax import lax
from jax.experimental import pallas as pl
from jax.experimental.pallas import tpu as pltpu
from jax.sharding import PartitionSpec as P

X, YH, YL, Z = 4, 2, 4, 8
Y = YH * YL
C = 2
MB, RT = 2, 16
TOK = MB * RT
SLOTS = 4 * C
LANES = 128
BLOCKS = (X // 2) * (Z // 2)
CC = BLOCKS * LANES
HID = 128
LOW = 8
MESH = pl.DeviceIdType.MESH
NT = (((1,), (1,)), ((), ()))


def dev(y, z, x, c):
    return (lax.div(y, YL) * Z + z) * X + x, lax.rem(y, YL) * C + c


def kernel(
    acts_hbm, dy_hbm, wg_hbm, wu_hbm, wd_hbm, ovf_hbm, out, rate_out,
    ovf, acts_v, dy_v, w_v, sx, sd, bx, bd, sw, wb, pt, pd, rx, rd, ab, hb, sz, rz, sy, ry, szd, rzd, syd, ryd, s2y, r2y, s2z, r2z,
    n1, m2, m3, ld, xs, xr, ds, dr, ws, wr, vs, vr, ps, pr, qs, qr, as_, ar, hs, hr, zs, zr, ys, yr, zds, zdr, yds, ydr, y2s, y2r, z2s, z2r,
    n1s, n1r, n2s, n2r, n3s, n3r,
):
    dp, t = lax.axis_index("dp"), lax.axis_index("tensor")
    x = lax.rem(dp, X)
    z = lax.rem(lax.div(dp, X), Z)
    yh = lax.div(dp, X * Z)
    yl = lax.div(t, C)
    c = lax.rem(t, C)
    y = yh * YL + yl
    sib = 1 - c
    px, pz = lax.rem(x, 2), lax.rem(z, 2)
    me = (px * 2 + pz) * C + c
    kme = lax.div(z, 2) * (X // 2) + lax.div(x, 2)

    even_x, even_z = x + 1 - 2 * px, z + 1 - 2 * pz
    odd_x, odd_z = lax.rem(x + X - 1 + 2 * px, X), lax.rem(z + Z - 1 + 2 * pz, Z)

    def even(ex, ez, core):
        return dev(y, even_z if ez else z, even_x if ex else x, core)

    def odd(ex, ez, core):
        return dev(y, odd_z if ez else z, odd_x if ex else x, core)

    def across(bit, flip):
        return 1 - bit if flip else bit

    def slot(ex, ez, ec):
        return (across(px, ex) * 2 + across(pz, ez)) * C + across(c, ec)

    def number(ex, ez, ec):
        return (ex * 2 + ez) * C + ec

    others = [(1, 1, 0), (1, 1, 1), (1, 0, 0), (0, 1, 0), (1, 0, 1), (0, 1, 1), (0, 0, 1)]

    loads = [
        pltpu.make_async_copy(src, dst, ld.at[i])
        for i, (src, dst) in enumerate(
            [
                (wg_hbm, w_v.at[0]),
                (wu_hbm, w_v.at[1]),
                (wd_hbm, w_v.at[2]),
                (acts_hbm, acts_v),
                (dy_hbm, dy_v),
                (ovf_hbm, ovf),
            ]
        )
    ]
    for load in loads:
        load.start()

    barrier = pltpu.get_barrier_semaphore()
    friends = [even(ex, ez, across(c, ec)) for ex, ez, ec in others]
    friends += [odd(ex, ez, across(c, ec)) for ex, ez, ec in others if ex or ez]
    for step in range(1, Y):
        for dc in range(C):
            friends.append(dev(lax.rem(y + step, Y), z, x, across(c, dc)))

    def class_dev(k):
        return dev(y, lax.div(k, X // 2) * 2 + pz, lax.rem(k, X // 2) * 2 + px, c)

    for friend in friends:
        pl.semaphore_signal(barrier, inc=1, device_id=friend, device_id_type=MESH)

    def columns(k, qx, qz, core):
        kz, kx = k // (X // 2), k % (X // 2)
        block = (core * Z + 2 * kz + qz) * X + 2 * kx + qx
        return pl.ds(pl.multiple_of(block * LANES, LANES), LANES)

    for load in loads[:3]:
        load.wait()
    for cp in range(C):
        for k in range(BLOCKS):
            sw[cp, :, :, k * LANES : (k + 1) * LANES] = w_v[:, :, columns(k, px, pz, cp)]
    pl.semaphore_wait(barrier, len(friends))

    sends = []

    def send(src, dst, send_sem, recv_sem, where):
        copy = pltpu.make_async_remote_copy(
            src_ref=src, dst_ref=dst, send_sem=send_sem, recv_sem=recv_sem, device_id=where, device_id_type=MESH
        )
        copy.start()
        return copy

    def arrived(dst, sem):
        pltpu.make_async_copy(dst, dst, sem).wait()

    same = c == yh

    def to_y(buf, slots, send_sems, recv_sems):
        for rel in range(1, YL * C):
            i = lax.rem(t + rel, YL * C)
            where = dev(c * YL + lax.div(i, C), z, x, lax.rem(i, C))
            sends.append(send(buf.at[i], slots.at[y], send_sems.at[rel], recv_sems.at[y], where))

        @pl.when(same)
        def _():
            slots[y] = buf[t]

        @pl.when(jnp.logical_not(same))
        def _():
            send(buf.at[t], slots.at[y], send_sems.at[0], recv_sems.at[y], dev(c * YL + yl, z, x, c))

    def from_y(buf, slots, send_sems, recv_sems):
        for rel in range(1, Y):
            arrived(slots.at[y], recv_sems.at[lax.rem(y + rel, Y)])

        @pl.when(jnp.logical_not(same))
        def _():
            arrived(slots.at[y], recv_sems.at[y])
            pltpu.make_async_copy(buf.at[t], buf.at[t], send_sems.at[0]).wait()

    near = [(0, 1), (1, 0), (1, 1), (3, 0), (3, 1)]
    far = [(2, 0), (2, 1)]

    def to_z(buf, slots, send_sems, recv_sems, steps):
        for kz, kx in steps:
            k = lax.rem(lax.div(z, 2) + kz, Z // 2) * 2 + across(lax.div(x, 2), kx)
            sends.append(send(buf.at[k], slots.at[kme], send_sems.at[kz * 2 + kx], recv_sems.at[kme], class_dev(k)))

    def from_z(slots, recv_sems):
        for rel in range(1, BLOCKS):
            arrived(slots.at[kme], recv_sems.at[lax.rem(kme + rel, BLOCKS)])

    def added(slots, length):
        value = slots[0].astype(jnp.float32)
        for n in range(1, length):
            value = value + slots[n].astype(jnp.float32)
        return value

    rows = pl.ds(pl.multiple_of(t * RT, RT), RT)
    half = CC // 2
    one, two = slice(0, half), slice(half, CC)
    up, down = slice(0, 2), slice(2, 3)
    routes = [(Y - 1, one), (1, two), (Y - 1, two), (1, one)]
    for i, (hop, cols) in enumerate(routes):
        for cp in range(C):
            where = dev(lax.rem(y + hop, Y), z, x, cp)
            n, to = i * C + cp, i * C + c
            sends.append(send(sw.at[cp, up, :, cols], wb.at[up, rows, cols], ws.at[n], wr.at[to], where))
    sends.append(send(sw.at[sib, up], wb.at[up, rows, :], ws.at[8], wr.at[8], dev(y, z, x, sib)))
    for load in loads[3:]:
        load.wait()
    for ex, ez, ec in others:
        n = number(ex, ez, ec)
        for k in range(BLOCKS):
            at = columns(k, across(px, ex), across(pz, ez), across(c, ec))
            sx[n, :, :, k * LANES : (k + 1) * LANES] = acts_v[:, :, at]
            sd[n, :, :, k * LANES : (k + 1) * LANES] = dy_v[:, :, at]
        sends.append(send(sx.at[n], bx.at[me], xs.at[n], xr.at[n], even(ex, ez, across(c, ec))))
        sends.append(send(sd.at[n], bd.at[me], ds.at[n], dr.at[n], odd(ex, ez, across(c, ec))))
    lost = (ovf[0, 0] + ovf[0, 1]).astype(jnp.float32)
    m3[yh] = jnp.full((8, LANES), lost, jnp.float32)
    sends.append(send(m3.at[yh], m3.at[yh], n3s, n3r, dev(lax.rem(y + YL, Y), z, x, c)))
    wb[:, rows, :] = sw[c]
    for k in range(BLOCKS):
        at = columns(k, px, pz, c)
        bx[me, :, :, k * LANES : (k + 1) * LANES] = acts_v[:, :, at]
        bd[me, :, :, k * LANES : (k + 1) * LANES] = dy_v[:, :, at]

    for i, (hop, cols) in enumerate(routes[:2]):
        for cp in range(C):
            arrived(wb.at[up, rows, cols], wr.at[i * C + cp])
        shard = pl.ds(pl.multiple_of(lax.rem(yl + YL - hop % YL, YL) * C * RT, C * RT), C * RT)
        where = dev(lax.rem(y + hop, Y), z, x, c)
        sends.append(send(wb.at[up, shard, cols], wb.at[up, shard, cols], ws.at[9 + i], wr.at[9 + i], where))
    hops = [(2, one), (Y - 2, two), (1, slice(0, CC)), (Y - 1, slice(0, CC))]
    for i, (hop, cols) in enumerate(hops):
        for cp in range(C):
            n, to, where = i * C + cp, i * C + c, dev(lax.rem(y + hop, Y), z, x, cp)
            sends.append(send(sw.at[cp, down, :, cols], wb.at[down, rows, cols], vs.at[n], vr.at[to], where))
    sends.append(send(sw.at[sib, down], wb.at[down, rows, :], vs.at[8], vr.at[8], dev(y, z, x, sib)))

    square = px * 2 + pz
    arrived(m3.at[yh], n3r)
    n1[square] = m3[0] + m3[1]
    for n, (ex, ez) in enumerate([(1, 1), (1, 0), (0, 1)]):
        sends.append(send(n1.at[square], n1.at[square], n1s.at[n], n1r.at[n], even(ex, ez, c)))

    pairs = [(1, 1), (1, 0), (0, 1), (0, 0)]
    for i, (hop, cols) in enumerate(routes[2:]):
        for cp in range(C):
            arrived(wb.at[up, rows, cols], wr.at[(2 + i) * C + cp])
    arrived(wb.at[up, rows, :], wr.at[8])
    for i, (hop, cols) in enumerate(routes[:2]):
        shard = pl.ds(0, C * RT)
        arrived(wb.at[up, shard, cols], wr.at[9 + i])
    for ex, ez in pairs:
        for ec in range(C):
            if ex or ez or ec:
                arrived(bx.at[me], xr.at[number(ex, ez, ec)])
        g = across(px, ex) * 2 + across(pz, ez)
        a = bx[pl.ds(g * C, C)].reshape(C * TOK, CC)
        gate_up = lax.dot_general(a, wb[0:2].reshape(2 * HID, CC), NT, preferred_element_type=jnp.float32)
        for cc in range(C):
            part = slice(cc * TOK, (cc + 1) * TOK)
            pt[g * C + cc, 0:TOK] = gate_up[part, :HID]
            pt[g * C + cc, TOK:] = gate_up[part, HID:]
        for ec in range(C):
            if ex or ez or ec:
                n, core = number(ex, ez, ec), across(c, ec)
                sends.append(send(pt.at[g * C + core], rx.at[me], ps.at[n], pr.at[n], even(ex, ez, core)))
    for i, (hop, cols) in enumerate(hops):
        for cp in range(C):
            arrived(wb.at[down, rows, cols], vr.at[i * C + cp])
    arrived(wb.at[down, rows, :], vr.at[8])
    for ex, ez in pairs:
        for ec in range(C):
            if ex or ez or ec:
                arrived(bd.at[me], dr.at[number(ex, ez, ec)])
        g = across(px, ex) * 2 + across(pz, ez)
        d = bd[pl.ds(g * C, C)].reshape(C * TOK, CC)
        dh = lax.dot_general(d, wb[2], NT, preferred_element_type=jnp.float32)
        for cc in range(C):
            pd[g * C + cc] = dh[cc * TOK : (cc + 1) * TOK]
        for ec in range(C):
            if ex or ez or ec:
                n, core = number(ex, ez, ec), across(c, ec)
                sends.append(send(pd.at[g * C + core], rd.at[me], qs.at[n], qr.at[n], odd(ex, ez, core)))
    rx[me] = pt[me]
    rd[me] = pd[me]
    for n in range(1, SLOTS):
        arrived(rx.at[me], pr.at[n])
    total = rx[0]
    for n in range(1, SLOTS):
        total = total + rx[n]
    gate, up = total[:TOK], total[TOK:]
    sig = 1.0 / (1.0 + jnp.exp(-gate))
    silu = gate * sig
    first = lax.broadcasted_iota(jnp.int32, (TOK, HID), 0) < RT
    keep_rows = jnp.where(first, 1 - ovf[0, 0], 1 - ovf[0, 1]) > 0
    zero = jnp.zeros((TOK, HID), jnp.float32)
    hb[me] = jnp.where(keep_rows, silu * up, zero).astype(jnp.bfloat16)
    for ex, ez, ec in others:
        n = number(ex, ez, ec)
        sends.append(send(hb.at[me], hb.at[me], hs.at[n], hr.at[n], odd(ex, ez, across(c, ec))))
    for n in range(1, SLOTS):
        arrived(rd.at[me], qr.at[n])
    dh = rd[0]
    for n in range(1, SLOTS):
        dh = dh + rd[n]
    ab[me, 0] = jnp.where(keep_rows, dh * up * sig * (1.0 + gate * (1.0 - sig)), zero).astype(jnp.bfloat16)
    ab[me, 1] = jnp.where(keep_rows, dh * silu, zero).astype(jnp.bfloat16)
    for ex, ez, ec in others:
        n = number(ex, ez, ec)
        sends.append(send(ab.at[me], ab.at[me], as_.at[n], ar.at[n], even(ex, ez, across(c, ec))))
    def products(lhs, tokens, low_buf, high_buf):
        wide = 2 * LANES
        for zt in range(BLOCKS // 2):
            cols = slice(zt * wide, (zt + 1) * wide)
            rhs = tokens[:, :, :, cols].reshape(SLOTS * TOK, wide)
            summed = jnp.dot(lhs, rhs, preferred_element_type=jnp.float32)
            for k in range(lhs.shape[0] // HID):
                block = summed[k * HID : (k + 1) * HID]
                pair = [block[:, :LANES], block[:, LANES:]]
                at = k * LOW * YL * C
                for b in range(2):
                    low = [pair[b][i * RT : i * RT + LOW] for i in range(YL * C)]
                    low_buf[zt * 2 + b, at : at + LOW * YL * C] = jnp.concatenate(low, axis=0).astype(jnp.bfloat16)
                at = k * 8 * BLOCKS + zt * 16
                for i in range(YL * C):
                    high = [p[i * RT + LOW : (i + 1) * RT] for p in pair]
                    high_buf[i, at : at + 16] = jnp.concatenate(high, axis=0).astype(jnp.bfloat16)

    for n in range(1, SLOTS):
        arrived(hb.at[me], hr.at[n])
    products(jnp.transpose(hb[...].reshape(SLOTS * TOK, HID)), bd, szd, syd)
    to_y(syd, ryd, yds, ydr)
    to_z(szd, rzd, zds, zdr, near)
    for n in range(1, SLOTS):
        arrived(ab.at[me], ar.at[n])
    to_z(szd, rzd, zds, zdr, far)
    rzd[kme] = szd[kme]
    lhs = [jnp.transpose(ab[:, k].reshape(SLOTS * TOK, HID)) for k in range(2)]
    products(jnp.concatenate(lhs, axis=0), bx, sz, sy)
    to_y(sy, ry, ys, yr)
    to_z(sz, rz, zs, zr, near + far)
    rz[kme] = sz[kme]
    for n in range(3):
        arrived(n1.at[square], n1r.at[n])
    m2[kme] = added(n1, 4)
    for rel in range(1, BLOCKS):
        k = lax.rem(kme + rel, BLOCKS)
        sends.append(send(m2.at[kme], m2.at[kme], n2s.at[rel], n2r.at[kme], class_dev(k)))
    from_y(syd, ryd, yds, ydr)
    high_down = added(ryd, Y)
    from_z(rzd, zdr)
    low_down = added(rzd, BLOCKS)
    from_y(sy, ry, ys, yr)
    high = (added(ry, Y), high_down)
    for k in range(BLOCKS):
        for m in range(3):
            at = m % 2 * 8 * BLOCKS + k * 8
            s2z[k, m * 8 : (m + 1) * 8] = high[m // 2][at : at + 8]
    to_z(s2z, r2z, z2s, z2r, near + far)
    r2z[kme] = s2z[kme]
    from_z(rz, zr)
    low = (added(rz, BLOCKS), low_down)
    for i in range(YL * C):
        for m in range(3):
            at = m % 2 * LOW * YL * C + i * LOW
            s2y[i, m * LOW : (m + 1) * LOW] = low[m // 2][at : at + LOW]
    to_y(s2y, r2y, y2s, y2r)
    from_z(r2z, z2r)
    high = added(r2z, BLOCKS)
    from_y(s2y, r2y, y2s, y2r)
    low = added(r2y, Y)
    from_z(m2, n2r)
    n_dp = lax.axis_size("dp")
    count = added(m2, BLOCKS)
    rate = 0.01 * (1.0 - count / jnp.float32(MB * n_dp))
    for m in range(3):
        out[m, 0:8] = low[m * 8 : (m + 1) * 8] / jnp.float32(MB * n_dp)
        out[m, 8:16] = high[m * 8 : (m + 1) * 8] / jnp.float32(MB * n_dp)
        rate_out[m, 0:8] = rate
        rate_out[m, 8:16] = rate

    for copy in sends:
        copy.wait_send()


def per_device(acts, grad_out, w_gate, w_up, w_down, overflow, step, master, moment1, moment2):
    d = acts.shape[2]
    bf16, f32 = jnp.bfloat16, jnp.float32
    dma = pltpu.SemaphoreType.DMA
    grad, rate = pl.pallas_call(
        kernel,
        out_shape=(jax.ShapeDtypeStruct((3, RT, LANES), f32),) * 2,
        in_specs=[pl.BlockSpec(memory_space=pl.ANY)] * 6,
        out_specs=(pl.BlockSpec(memory_space=pltpu.VMEM),) * 2,
        scratch_shapes=[
            pltpu.SMEM((1, MB), jnp.int32),
            pltpu.VMEM((MB, RT, d), bf16),
            pltpu.VMEM((MB, RT, d), bf16),
            pltpu.VMEM((3, RT, d), bf16),
            pltpu.VMEM((SLOTS, MB, RT, CC), bf16),
            pltpu.VMEM((SLOTS, MB, RT, CC), bf16),
            pltpu.VMEM((SLOTS, MB, RT, CC), bf16),
            pltpu.VMEM((SLOTS, MB, RT, CC), bf16),
            pltpu.VMEM((C, 3, RT, CC), bf16),
            pltpu.VMEM((3, HID, CC), bf16),
            pltpu.VMEM((SLOTS, 2 * TOK, LANES), f32),
            pltpu.VMEM((SLOTS, TOK, LANES), f32),
            pltpu.VMEM((SLOTS, 2 * TOK, LANES), f32),
            pltpu.VMEM((SLOTS, TOK, LANES), f32),
            pltpu.VMEM((SLOTS, 2, TOK, HID), bf16),
            pltpu.VMEM((SLOTS, TOK, HID), bf16),
            pltpu.VMEM((BLOCKS, 2 * LOW * YL * C, LANES), bf16),
            pltpu.VMEM((BLOCKS, 2 * LOW * YL * C, LANES), bf16),
            pltpu.VMEM((YL * C, 2 * 8 * BLOCKS, LANES), bf16),
            pltpu.VMEM((Y, 2 * 8 * BLOCKS, LANES), bf16),
            pltpu.VMEM((BLOCKS, LOW * YL * C, LANES), bf16),
            pltpu.VMEM((BLOCKS, LOW * YL * C, LANES), bf16),
            pltpu.VMEM((YL * C, 8 * BLOCKS, LANES), bf16),
            pltpu.VMEM((Y, 8 * BLOCKS, LANES), bf16),
            pltpu.VMEM((YL * C, 3 * LOW, LANES), f32),
            pltpu.VMEM((Y, 3 * LOW, LANES), f32),
            pltpu.VMEM((BLOCKS, 24, LANES), f32),
            pltpu.VMEM((BLOCKS, 24, LANES), f32),
            pltpu.VMEM((4, 8, LANES), f32),
            pltpu.VMEM((BLOCKS, 8, LANES), f32),
            pltpu.VMEM((YH, 8, LANES), f32),
            dma((6,)),
            dma((SLOTS,)), dma((SLOTS,)),
            dma((SLOTS,)), dma((SLOTS,)),
            dma((11,)), dma((11,)),
            dma((9,)), dma((9,)),
            dma((SLOTS,)), dma((SLOTS,)),
            dma((SLOTS,)), dma((SLOTS,)),
            dma((SLOTS,)), dma((SLOTS,)),
            dma((SLOTS,)), dma((SLOTS,)),
            dma((BLOCKS,)), dma((BLOCKS,)),
            dma((Y,)), dma((Y,)),
            dma((BLOCKS,)), dma((BLOCKS,)),
            dma((Y,)), dma((Y,)),
            dma((Y,)), dma((Y,)),
            dma((BLOCKS,)), dma((BLOCKS,)),
            dma((3,)), dma((3,)),
            dma((BLOCKS,)), dma((BLOCKS,)),
            dma, dma,
        ],
        compiler_params=pltpu.CompilerParams(
            collective_id=0, has_side_effects=True, vmem_limit_bytes=63 * 1024 * 1024
        ),
        name="window_grads",
    )(acts, grad_out, w_gate.T, w_up.T, w_down, overflow)
    new_moment1 = 0.9 * moment1 + 0.1 * grad
    new_moment2 = 0.95 * moment2 + 0.05 * grad * grad
    steps_f = step[0].astype(f32)
    corr1 = 1.0 - jnp.power(f32(0.9), steps_f)
    corr2 = 1.0 - jnp.power(f32(0.95), steps_f)
    direction = new_moment1 / corr1 / (jnp.sqrt(new_moment2 / corr2) + 1e-08)
    new_master = master - rate * (direction + 0.1 * master)
    return (new_master, new_moment1, new_moment2)


def solution(mesh):
    in_specs = (
        P(None, ("dp", "tensor"), None),
        P(None, ("dp", "tensor"), None),
        P(None, "tensor"),
        P(None, "tensor"),
        P("tensor", None),
        P("dp", None),
        P(),
        P(None, "tensor", "dp"),
        P(None, "tensor", "dp"),
        P(None, "tensor", "dp"),
    )
    out_specs = (P(None, "tensor", "dp"), P(None, "tensor", "dp"), P(None, "tensor", "dp"))
    return jax.shard_map(
        per_device, mesh=mesh, in_specs=in_specs, out_specs=out_specs, check_vma=False
    )
```
